32 devices in a mesh: section: 16 (over z, y, x), tp: 2 (over core).
Axes of the slice: x: 2, y: 2, z: 4, core: 2. Of those that a mesh axis runs over, the one named last changes fastest.
Arguments:
- queries: bfloat16 [6144, 3072], P('section', 'tp'), may hold values from -60 to 60
- keys: bfloat16 [6144, 3072], P('section', 'tp'), may hold values from -6 to 6
- values: bfloat16 [6144, 3072], P('section', 'tp'), may hold values from -40 to 40
- cotangent: bfloat16 [6144, 3072], P('section', 'tp'), may hold values from -6 to 6
- doc_ids: int32 [6144], P('section'), may hold values from 0 to 3, never falling along the last dimension, each value on 1 to 3072 neighbouring positions
- gain: float32 [3072], P('tp'), may hold values from 0.1 to 1.9
Outputs:
- normed: bfloat16 [6144, 3072], P('section', 'tp')
- grad_queries: bfloat16 [6144, 3072], P('section', 'tp')
- grad_keys: bfloat16 [6144, 3072], P('section', 'tp')
- grad_values: bfloat16 [6144, 3072], P('section', 'tp')
The draws below stay inside these ranges and needn't reach their ends.
All inputs are finite; a program needn't handle non-finite values.
Results may differ from the reference program's by a relative error of at most 0.009.
Values may be sent and summed in bfloat16 or wider, within the bound.
A program may use at most 192 MiB of HBM per device.

```python
import math
import jax
import jax.numpy as jnp
import numpy as np
from jax import lax

HS = 128
TOK_DEV = 384
BAND_DEV = 2
HEADS = 24
F = 3072
SEQ = 6144
WIN = 768
DOCS = 4
DOC_MOST = 3072
N_SECTION = 16


def draw_queries(key, part):
    key = jax.random.fold_in(key, 11)
    first_key = jax.random.fold_in(key, 0)
    drawn = jnp.clip(jax.random.normal(first_key, (SEQ, F), jnp.float32), -6.0, 6.0)
    return drawn.astype(jnp.bfloat16)


def draw_keys(key, part):
    key = jax.random.fold_in(key, 23)
    drawn = jnp.clip(jax.random.normal(key, (SEQ, F), jnp.float32), -6.0, 6.0)
    return drawn.astype(jnp.bfloat16)


def draw_values(key, part):
    key = jax.random.fold_in(key, 37)
    first_key, second_key = jax.random.split(key)
    column_ramp = jnp.arange(F, dtype=jnp.float32) / max(F - 1, 1)
    base_part = jnp.clip(jax.random.normal(first_key, (SEQ, F), jnp.float32), -6.0, 6.0)
    column_scale = jnp.exp(column_ramp * jnp.log(3.0)) / jnp.sqrt(3.0)
    row_scale = jnp.exp(jax.random.uniform(second_key, (SEQ, 1), jnp.float32, jnp.log(0.32), jnp.log(3.2)))
    drawn = base_part * column_scale[None, :] * row_scale
    return drawn.astype(jnp.bfloat16)


def levels(stream_key, extent, cuts, low, top_value):
    def one(position, shards_of):
        steps = jax.random.uniform(jax.random.fold_in(jax.random.fold_in(stream_key, 6), position), (shards_of,), jnp.float32, low / len(cuts), top_value / len(cuts))
        return jnp.repeat(jnp.exp(steps), extent[position] // shards_of).reshape((-1,) + (1,) * (len(extent) - position - 1))

    factor_of = one(*cuts[0])
    for cut in cuts[1:]:
        factor_of = factor_of * one(*cut)
    return factor_of


def split_up(count, total, most, lean):
    weights = [(1 << 20) // math.isqrt(rank ** lean) + 1 for rank in range(2, count + 1)]
    spare, given = total - most - (count - 1), [1] * (count - 1)
    while spare > 0:
        movable = [i for i in range(count - 1) if given[i] < most]
        pool, left = sum([weights[i] for i in movable]), spare
        for i in movable:
            addition = min(most - given[i], max(1, left * weights[i] // pool), spare)
            given[i] = given[i] + addition
            spare = spare - addition
    return np.array([most] + given)


def uneven_parts(stream_key, number_of, total, most, skew):
    if number_of == 2:
        one = jax.random.randint(stream_key, (), max(1, total - most), min(most, total - 1) + 1)
        return jnp.stack([one, total - one])
    lengths = jnp.asarray(split_up(number_of, total, most, skew), jnp.int32)
    couples = (number_of - 1) // 2
    donor, sink = lengths[1:1 + 2 * couples:2], lengths[2:2 + 2 * couples:2]
    slack = jnp.minimum(donor - 1, most - sink)
    shifted = jax.random.randint(jax.random.fold_in(stream_key, 1), (couples,), 0, 1 << 20) % (slack + 1)
    lengths = lengths.at[1:1 + 2 * couples:2].set(donor - shifted).at[2:2 + 2 * couples:2].set(sink + shifted)
    return lengths[jax.random.permutation(jax.random.fold_in(stream_key, 2), number_of)]


def gaussian(rng, extent, width, bound, cuts=(), kind=jnp.bfloat16):
    result = jax.random.normal(rng, extent, jnp.float32) * width
    if len(cuts) > 0:
        result = levels(rng, extent, cuts, -0.22, 0.18) * result
    return jnp.clip(result, min=-bound, max=bound).astype(kind)


def setup_inputs(seed: int = 0) -> dict:
    key_list = jax.random.split(jax.random.key(seed), 7)
    queries = draw_queries(jax.random.fold_in(key_list[6], 71), 0)
    keys = draw_keys(jax.random.fold_in(key_list[6], 71), 0)
    values = draw_values(jax.random.fold_in(key_list[6], 71), 0)
    cotangent = gaussian(key_list[3], (SEQ, F), 1.0, 6.0, ((0, 16), (1, 2)))
    doc_ids = jnp.searchsorted(jnp.cumsum(uneven_parts(key_list[4], DOCS, SEQ, DOC_MOST, 0)), jnp.arange(SEQ), side="right").astype(jnp.int32)
    gain = jnp.clip(1.0 + 0.18 * jax.random.normal(key_list[5], (F,), jnp.float32), 0.1, 1.9)
    return {"queries": queries, "keys": keys, "values": values, "cotangent": cotangent, "doc_ids": doc_ids, "gain": gain}


def band_mask(query_pos, query_doc, key_pos, key_doc, window):
    distance = query_pos[:, None] - key_pos[None, :]
    return (distance >= 0) & (distance < window) & (key_pos[None, :] >= 0) & (query_doc[:, None] == key_doc[None, :])

def reference(queries, keys, values, cotangent, doc_ids, gain):
    margin = BAND_DEV * TOK_DEV
    span = (BAND_DEV + 1) * TOK_DEV
    score_scale = HS ** (-0.5)
    key_pad = jnp.concatenate([jnp.zeros((margin, F), keys.dtype), keys], 0)
    value_pad = jnp.concatenate([jnp.zeros((margin, F), values.dtype), values], 0)
    doc_pad = jnp.concatenate([-jnp.ones((margin,), jnp.int32), doc_ids], 0)
    offsets = jnp.arange(TOK_DEV, dtype=jnp.int32)
    band_offsets = jnp.arange(span, dtype=jnp.int32)

    def gather_band(block):
        start = (block * TOK_DEV).astype(jnp.int32)
        query_block = lax.dynamic_slice_in_dim(queries, start, TOK_DEV, 0).reshape(TOK_DEV, HEADS, HS).astype(jnp.float32)
        key_band = lax.dynamic_slice_in_dim(key_pad, start, span, 0).reshape(span, HEADS, HS).astype(jnp.float32)
        value_band = lax.dynamic_slice_in_dim(value_pad, start, span, 0).reshape(span, HEADS, HS).astype(jnp.float32)
        query_doc = lax.dynamic_slice_in_dim(doc_ids, start, TOK_DEV, 0)
        key_doc = lax.dynamic_slice_in_dim(doc_pad, start, span, 0)
        visible = band_mask(start + offsets, query_doc, start - margin + band_offsets, key_doc, WIN)
        scores = jnp.einsum('qhd,khd->hqk', query_block, key_band) * score_scale
        scores = jnp.where(visible[None], scores, -1e+30)
        return (start, query_block, key_band, value_band, scores)

    def forward(block):
        start, query_block, key_band, value_band, scores = gather_band(block)
        row_max = lax.optimization_barrier(jnp.max(scores, axis=-1, keepdims=True))
        log_total = row_max + jnp.log(lax.optimization_barrier(jnp.sum(jnp.exp(scores - row_max), axis=-1, keepdims=True)))
        weights_b = jnp.exp(scores - log_total).astype(jnp.bfloat16).astype(jnp.float32)
        attended = jnp.einsum('hqk,khd->qhd', weights_b, value_band)
        return (attended.reshape(TOK_DEV, F), log_total[:, :, 0])
    blocks = jnp.arange(N_SECTION, dtype=jnp.int32)
    attended, log_totals = lax.map(forward, blocks)
    attended = attended.reshape(SEQ, F)
    inverse = lax.rsqrt(lax.optimization_barrier(jnp.sum(attended * attended, axis=-1, keepdims=True)) / F + 1e-05)
    normed = (attended * inverse * gain).astype(jnp.bfloat16)
    scaled_grad = cotangent.astype(jnp.float32) * gain
    inner_sum = lax.optimization_barrier(jnp.sum(scaled_grad * attended, axis=-1, keepdims=True))
    grad_out = (inverse * scaled_grad - attended * inverse ** 3 * inner_sum / F).astype(jnp.bfloat16)
    row_delta = lax.optimization_barrier(jnp.sum(grad_out.astype(jnp.float32).reshape(SEQ, HEADS, HS) * attended.reshape(SEQ, HEADS, HS), axis=-1))

    def backward(carry, block):
        grad_key_pad, grad_value_pad = carry
        start, query_block, key_band, value_band, scores = gather_band(block)
        log_block = lax.dynamic_index_in_dim(log_totals, block, 0, keepdims=False)
        weights = jnp.exp(scores - log_block[:, :, None])
        weights_b = weights.astype(jnp.bfloat16).astype(jnp.float32)
        grad_block = lax.dynamic_slice_in_dim(grad_out, start, TOK_DEV, 0).reshape(TOK_DEV, HEADS, HS).astype(jnp.float32)
        delta_block = lax.dynamic_slice_in_dim(row_delta, start, TOK_DEV, 0).T
        grad_weights = jnp.einsum('qhd,khd->hqk', grad_block, value_band)
        dscore = (weights * (grad_weights - delta_block[:, :, None])).astype(jnp.bfloat16).astype(jnp.float32)
        grad_query = jnp.einsum('hqk,khd->qhd', dscore, key_band) * score_scale
        key_part = (jnp.einsum('hqk,qhd->khd', dscore, query_block) * score_scale).reshape(span, F)
        value_part = jnp.einsum('hqk,qhd->khd', weights_b, grad_block).reshape(span, F)
        grad_key_pad = lax.dynamic_update_slice_in_dim(grad_key_pad, lax.dynamic_slice_in_dim(grad_key_pad, start, span, 0) + key_part, start, 0)
        grad_value_pad = lax.dynamic_update_slice_in_dim(grad_value_pad, lax.dynamic_slice_in_dim(grad_value_pad, start, span, 0) + value_part, start, 0)
        return ((grad_key_pad, grad_value_pad), grad_query.reshape(TOK_DEV, F))
    empty = jnp.zeros((SEQ + margin, F), jnp.float32)
    (grad_key_pad, grad_value_pad), grad_queries = lax.scan(backward, (empty, empty), blocks)
    grad_queries = grad_queries.reshape(SEQ, F).astype(jnp.bfloat16)
    grad_keys = grad_key_pad[margin:].astype(jnp.bfloat16)
    grad_values = grad_value_pad[margin:].astype(jnp.bfloat16)
    return (normed, grad_queries, grad_keys, grad_values)
```

```python
import functools
import math

import jax
import jax.numpy as jnp
from jax import lax
from jax.experimental import pallas as pl
from jax.experimental.pallas import tpu as pltpu
from jax.sharding import PartitionSpec as P

HS = 128
GROUPS = 4
MESH = pl.DeviceIdType.MESH
LOG2E = math.log2(math.e)
HIDDEN = -1e30
NT = (((1,), (1,)), ((), ()))


def nt_dot(a, b):
    return lax.dot_general(a, b, NT, preferred_element_type=jnp.float32)


def nn_dot(a, b):
    return jnp.dot(a, b, preferred_element_type=jnp.float32)


def kernel(
    n,
    tp,
    q_ref,
    k_ref,
    v_ref,
    cot_ref,
    doc_ref,
    gain_ref,
    normed_ref,
    dq_ref,
    dk_ref,
    dv_ref,
    kv_buf,
    qo_buf,
    do_ref,
    att_ref,
    w_ref,
    bias_ref,
    bias_t_ref,
    dk_acc,
    dv_acc,
    doc_own,
    doc_buf,
    sums,
    sums_buf,
    stat_col,
    stat_own,
    stat_buf,
    kv_send,
    kv_recv,
    qo_send,
    qo_recv,
    doc_send,
    doc_recv,
    sums_send,
    sums_recv,
    stat_send,
    stat_recv,
):
    rows, cols = q_ref.shape
    heads = cols // HS
    per_group = heads // GROUPS
    width = per_group * HS
    features = cols * tp
    scale = HS ** (-0.5)
    scale2 = scale * LOG2E
    hp = stat_own.shape[1]
    s = lax.axis_index("section")
    t = lax.axis_index("tp")
    odd = lax.rem(s, 2) == 1
    even = lax.rem(s, 2) == 0

    def copy(src, dst, send, recv, section):
        return pltpu.make_async_remote_copy(
            src_ref=src,
            dst_ref=dst,
            send_sem=send,
            recv_sem=recv,
            device_id={"section": section},
            device_id_type=MESH,
        )

    def group_cols(g):
        return pl.ds(pl.multiple_of(g * width, HS), width)

    def head_cols(h):
        return pl.ds(pl.multiple_of(h * HS, HS), HS)

    near = [(-1, s >= 1), (-2, s >= 2), (1, s + 1 < n), (2, s + 2 < n)]

    barrier = pltpu.get_barrier_semaphore()
    for step, there in near:
        @pl.when(there)
        def _():
            pl.semaphore_signal(
                barrier, inc=1, device_id={"section": s + step}, device_id_type=MESH
            )
    for j in range(1, tp):
        pl.semaphore_signal(
            barrier, inc=1, device_id={"tp": lax.rem(t + j, tp)}, device_id_type=MESH
        )
    pl.semaphore_wait(barrier, jnp.minimum(s, 2) + jnp.minimum(n - 1 - s, 2) + tp - 1)

    doc_own[...] = jnp.broadcast_to(doc_ref[...], doc_own.shape)
    back = [2, 3, 0, 1]

    def doc_copy(i):
        return copy(
            doc_own, doc_buf.at[back[i]], doc_send.at[i], doc_recv.at[back[i]], s + near[i][0]
        )

    for i in range(4):
        @pl.when(near[i][1])
        def _():
            doc_copy(i).start()

    kv_src = (k_ref, v_ref)
    qo_src = (q_ref, do_ref)

    def kv_copy(a, slot, g, src, section):
        c = group_cols(g)
        return copy(
            src.at[:, c], kv_buf.at[a, slot, :, c], kv_send.at[a, slot, g],
            kv_recv.at[a, slot, g], section,
        )

    def qo_copy(a, slot, g, src, section):
        c = group_cols(g)
        return copy(
            src.at[:, c], qo_buf.at[a, slot, :, c], qo_send.at[a, slot, g],
            qo_recv.at[a, slot, g], section,
        )

    def kv_start(g):
        for a in range(2):
            @pl.when(even)
            def _():
                kv_copy(a, 0, g, kv_src[a], s + 1).start()

            @pl.when(s + 2 < n)
            def _():
                kv_copy(a, 1, g, kv_src[a], s + 2).start()

    def qo_start(a, g):
        @pl.when(odd)
        def _():
            qo_copy(a, 0, g, qo_src[a], s - 1).start()

        @pl.when(s >= 2)
        def _():
            qo_copy(a, 1, g, qo_src[a], s - 2).start()

    def kv_arrive(g):
        @pl.when(s >= 2)
        def _():
            for a in range(2):
                kv_copy(a, 1, g, kv_src[a], s).wait_recv()

                @pl.when(odd)
                def _():
                    kv_copy(a, 0, g, kv_buf.at[a, 1], s - 1).start()

        @pl.when(s >= 1)
        def _():
            for a in range(2):
                kv_copy(a, 0, g, kv_src[a], s).wait_recv()

    def qo_far_arrive(g):
        @pl.when(s + 2 < n)
        def _():
            for a in range(2):
                qo_copy(a, 1, g, qo_src[a], s).wait_recv()

                @pl.when(even)
                def _():
                    qo_copy(a, 0, g, qo_buf.at[a, 1], s + 1).start()

    def qo_near_arrive(g):
        @pl.when(s + 1 < n)
        def _():
            for a in range(2):
                qo_copy(a, 0, g, qo_src[a], s).wait_recv()

    def loop(count, f):
        lax.fori_loop(0, count, lambda i, c: (f(i), c)[1], 0)

    loop(GROUPS, kv_start)

    for slot in range(2):
        @pl.when(s < slot + 1)
        def _():
            kv_buf[:, slot] = jnp.zeros((2, rows, cols), kv_buf.dtype)
            doc_buf[slot] = jnp.zeros(doc_buf.shape[1:], doc_buf.dtype)

        @pl.when(s + slot + 1 >= n)
        def _():
            qo_buf[:, slot] = jnp.zeros((2, rows, cols), qo_buf.dtype)
            stat_buf[slot] = jnp.zeros(stat_buf.shape[1:], stat_buf.dtype)
            doc_buf[2 + slot] = jnp.zeros(doc_buf.shape[1:], doc_buf.dtype)

    sums[...] = jnp.zeros(sums.shape, sums.dtype)
    stat_col[...] = jnp.zeros(stat_col.shape, stat_col.dtype)

    doc_row = doc_ref[...].astype(jnp.float32)
    doc_col = jnp.transpose(jnp.broadcast_to(doc_row, (HS, rows)))[:, :1]
    for i in range(4):
        @pl.when(near[i][1])
        def _():
            doc_copy(i).wait_send()
            copy(doc_own, doc_buf.at[i], doc_send.at[i], doc_recv.at[i], s).wait_recv()
    down = lax.broadcasted_iota(jnp.int32, (rows, rows), 0)
    across = lax.broadcasted_iota(jnp.int32, (rows, rows), 1)

    def bias(visible):
        return jnp.where(visible, 0.0, HIDDEN)

    same = doc_col == doc_row
    bias_ref[0] = bias(same & (down >= across))
    bias_t_ref[0] = bias(same & (across >= down))
    for i in range(2):
        for ref, slot, where_far in ((bias_ref, i, down < across), (bias_t_ref, i + 2, across < down)):
            other = doc_buf[slot][:1].astype(jnp.float32)
            visible = (doc_col == other) & near[slot][1]
            if i == 1:
                visible = visible & where_far
            ref[i + 1] = bias(visible)

    lane = lax.broadcasted_iota(jnp.int32, (rows, HS), 1)

    def keys_of(j, c):
        return k_ref[:, c] if j == 0 else kv_buf[0, j - 1, :, c]

    def values_of(j, c):
        return v_ref[:, c] if j == 0 else kv_buf[1, j - 1, :, c]

    def forward_head(h):
        c = head_cols(h)
        q = q_ref[:, c]
        scores = [nt_dot(q, keys_of(j, c)) * scale2 + bias_ref[j] for j in range(3)]
        top = jnp.max(
            jnp.maximum(jnp.maximum(scores[0], scores[1]), scores[2]), axis=-1, keepdims=True
        )
        parts = [jnp.exp2(x - top) for x in scores]
        total = jnp.sum(parts[0] + parts[1] + parts[2], axis=-1, keepdims=True)
        recip = 1.0 / total
        att = jnp.zeros((rows, HS), jnp.float32)
        for j in range(3):
            w = (parts[j] * recip).astype(jnp.bfloat16)
            w_ref[h, :, j * rows : (j + 1) * rows] = w
            att = att + nn_dot(w, values_of(j, c))
        att_ref[:, c] = att
        stat_col[0] = jnp.where(lane == h, top + jnp.log2(total), stat_col[0])
        sums[0] += att * att
        sums[1] += cot_ref[:, c].astype(jnp.float32) * gain_ref[:, c] * att

    def forward_group(g):
        kv_arrive(g)
        qo_start(0, g)
        loop(per_group, lambda i: forward_head(g * per_group + i))

    loop(GROUPS, forward_group)

    def sums_copy(j):
        return pltpu.make_async_remote_copy(
            src_ref=sums,
            dst_ref=sums_buf.at[j - 1],
            send_sem=sums_send.at[j - 1],
            recv_sem=sums_recv.at[j - 1],
            device_id={"tp": lax.rem(t + j, tp)},
            device_id_type=MESH,
        )

    for j in range(1, tp):
        sums_copy(j).start()
    squares, inner = sums[0], sums[1]
    for j in range(1, tp):
        sums_copy(j).wait()
        squares = squares + sums_buf[j - 1, 0]
        inner = inner + sums_buf[j - 1, 1]
    inverse = lax.rsqrt(jnp.sum(squares, axis=-1, keepdims=True) / features + 1e-05)
    factor = inverse * inverse * inverse * jnp.sum(inner, axis=-1, keepdims=True) / features
    sums[0] = jnp.broadcast_to(inverse, (rows, HS))
    sums[1] = jnp.broadcast_to(factor, (rows, HS))

    def norm_head(h):
        c = head_cols(h)
        att = att_ref[:, c]
        gain = gain_ref[:, c]
        normed_ref[:, c] = (att * sums[0] * gain).astype(normed_ref.dtype)
        grad = sums[0] * (cot_ref[:, c].astype(jnp.float32) * gain) - att * sums[1]
        grad = grad.astype(do_ref.dtype)
        do_ref[:, c] = grad
        delta = jnp.sum(grad.astype(jnp.float32) * att, axis=-1, keepdims=True)
        stat_col[1] = jnp.where(lane == h, delta, stat_col[1])

    def norm_group(g):
        loop(per_group, lambda i: norm_head(g * per_group + i))
        qo_start(1, g)

    loop(GROUPS, norm_group)
    for i in range(2):
        stat_own[i] = jnp.transpose(stat_col[i])[:hp]

    def stat_copy(slot):
        return copy(
            stat_own, stat_buf.at[slot], stat_send.at[slot], stat_recv.at[slot], s - slot - 1
        )

    for slot in range(2):
        @pl.when(s >= slot + 1)
        def _():
            stat_copy(slot).start()
    for slot in range(2):
        @pl.when(s + slot + 1 < n)
        def _():
            copy(
                stat_own, stat_buf.at[slot], stat_send.at[slot], stat_recv.at[slot], s
            ).wait_recv()

    def query_head(h):
        c = head_cols(h)
        grad = do_ref[:, c]
        delta = jnp.sum(grad.astype(jnp.float32) * att_ref[:, c], axis=-1, keepdims=True)
        dq = jnp.zeros((rows, HS), jnp.float32)
        for j in range(3):
            w = w_ref[h, :, j * rows : (j + 1) * rows].astype(jnp.float32)
            ds = (w * (nt_dot(grad, values_of(j, c)) - delta)).astype(jnp.bfloat16)
            dq = dq + nn_dot(ds, keys_of(j, c))
        dq_ref[:, c] = (dq * scale).astype(dq_ref.dtype)

    def key_terms(h, j):
        c = head_cols(h)
        if j == 0:
            q, grad = q_ref[:, c], do_ref[:, c]
            log_total, delta = stat_own[0, pl.ds(h, 1), :], stat_own[1, pl.ds(h, 1), :]
        else:
            q, grad = qo_buf[0, j - 1, :, c], qo_buf[1, j - 1, :, c]
            log_total = stat_buf[j - 1, 0, pl.ds(h, 1), :]
            delta = stat_buf[j - 1, 1, pl.ds(h, 1), :]
        w = jnp.exp2(nt_dot(k_ref[:, c], q) * scale2 + bias_t_ref[j] - log_total)
        ds = (w * (nt_dot(v_ref[:, c], grad) - delta)).astype(jnp.bfloat16)
        return nn_dot(ds, q), nn_dot(w.astype(jnp.bfloat16), grad)

    def early_head(h):
        c = head_cols(h)
        query_head(h)
        own, far_one = key_terms(h, 0), key_terms(h, 2)
        dk_acc[:, c] = own[0] + far_one[0]
        dv_acc[:, c] = own[1] + far_one[1]

    def late_head(h):
        c = head_cols(h)
        dk, dv = key_terms(h, 1)
        dk_ref[:, c] = ((dk_acc[:, c] + dk) * scale).astype(dk_ref.dtype)
        dv_ref[:, c] = (dv_acc[:, c] + dv).astype(dv_ref.dtype)

    def backward_step(g):
        @pl.when(g < GROUPS)
        def _():
            qo_far_arrive(g)
            loop(per_group, lambda i: early_head(g * per_group + i))

        @pl.when(g >= 1)
        def _():
            qo_near_arrive(g - 1)
            loop(per_group, lambda i: late_head((g - 1) * per_group + i))

    loop(GROUPS + 1, backward_step)

    for slot in range(2):
        @pl.when(s >= slot + 1)
        def _():
            stat_copy(slot).wait_send()

    def sent(g):
        for a in range(2):
            @pl.when(even | (s >= 3))
            def _():
                kv_copy(a, 0, g, kv_src[a], s).wait_send()

            @pl.when(s + 2 < n)
            def _():
                kv_copy(a, 1, g, kv_src[a], s).wait_send()

            @pl.when(odd | (s + 3 < n))
            def _():
                qo_copy(a, 0, g, qo_src[a], s).wait_send()

            @pl.when(s >= 2)
            def _():
                qo_copy(a, 1, g, qo_src[a], s).wait_send()

    loop(GROUPS, sent)


def body(n, tp, queries, keys, values, cotangent, doc_ids, gain):
    rows, cols = queries.shape
    heads = cols // HS
    hp = -(-heads // 8) * 8
    vmem = pl.BlockSpec(memory_space=pltpu.VMEM)
    bf16, f32 = jnp.bfloat16, jnp.float32
    dma = pltpu.SemaphoreType.DMA
    out = jax.ShapeDtypeStruct((rows, cols), bf16)
    return pl.pallas_call(
        functools.partial(kernel, n, tp),
        out_shape=(out,) * 4,
        in_specs=[vmem] * 6,
        out_specs=(vmem,) * 4,
        scratch_shapes=[
            pltpu.VMEM((2, 2, rows, cols), bf16),
            pltpu.VMEM((2, 2, rows, cols), bf16),
            pltpu.VMEM((rows, cols), bf16),
            pltpu.VMEM((rows, cols), f32),
            pltpu.VMEM((heads, rows, 3 * rows), bf16),
            pltpu.VMEM((3, rows, rows), f32),
            pltpu.VMEM((3, rows, rows), f32),
            pltpu.VMEM((rows, cols), f32),
            pltpu.VMEM((rows, cols), f32),
            pltpu.VMEM((8, rows), jnp.int32),
            pltpu.VMEM((4, 8, rows), jnp.int32),
            pltpu.VMEM((2, rows, HS), f32),
            pltpu.VMEM((max(tp - 1, 1), 2, rows, HS), f32),
            pltpu.VMEM((2, rows, HS), f32),
            pltpu.VMEM((2, hp, rows), f32),
            pltpu.VMEM((2, 2, hp, rows), f32),
            dma((2, 2, GROUPS)),
            dma((2, 2, GROUPS)),
            dma((2, 2, GROUPS)),
            dma((2, 2, GROUPS)),
            dma((4,)),
            dma((4,)),
            dma((max(tp - 1, 1),)),
            dma((max(tp - 1, 1),)),
            dma((2,)),
            dma((2,)),
        ],
        compiler_params=pltpu.CompilerParams(
            collective_id=0, has_side_effects=True, vmem_limit_bytes=60 * 1024 * 1024
        ),
        cost_estimate=pl.CostEstimate(
            flops=16 * heads * 3 * rows * rows * HS,
            bytes_accessed=16 * rows * cols,
            transcendentals=6 * heads * rows * rows,
        ),
    )(queries, keys, values, cotangent, doc_ids.reshape(1, rows), gain.reshape(1, cols))


def solution(mesh):
    wide = P("section", "tp")
    return jax.shard_map(
        functools.partial(body, mesh.shape["section"], mesh.shape["tp"]),
        mesh=mesh,
        in_specs=(wide, wide, wide, wide, P("section"), P("tp")),
        out_specs=(wide,) * 4,
        check_vma=False,
    )
```

```python
import functools
import math

import jax
import jax.numpy as jnp
from jax import lax
from jax.experimental import pallas as pl
from jax.experimental.pallas import tpu as pltpu
from jax.sharding import PartitionSpec as P

HS = 128
GROUPS = 6
MESH = pl.DeviceIdType.MESH
LOG2E = math.log2(math.e)
HIDDEN = -1e30
NT = (((1,), (1,)), ((), ()))


def nt_dot(a, b):
    return lax.dot_general(a, b, NT, preferred_element_type=jnp.float32)


def nn_dot(a, b):
    return jnp.dot(a, b, preferred_element_type=jnp.float32)


def kernel(
    n,
    tp,
    q_ref,
    k_ref,
    v_ref,
    cot_ref,
    doc_ref,
    gain_ref,
    normed_ref,
    dq_ref,
    dk_ref,
    dv_ref,
    kv_buf,
    qo_buf,
    do_ref,
    att_ref,
    w_ref,
    bias_ref,
    bias_t_ref,
    dk_acc,
    dv_acc,
    doc_own,
    doc_buf,
    sums,
    sums_buf,
    stat_col,
    stat_own,
    stat_buf,
    kv_send,
    kv_recv,
    qo_send,
    qo_recv,
    doc_send,
    doc_recv,
    sums_send,
    sums_recv,
    stat_send,
    stat_recv,
):
    rows, cols = q_ref.shape
    heads = cols // HS
    per_group = heads // GROUPS
    width = per_group * HS
    features = cols * tp
    scale = HS ** (-0.5)
    scale2 = scale * LOG2E
    hp = stat_own.shape[1]
    s = lax.axis_index("section")
    t = lax.axis_index("tp")
    odd = lax.rem(s, 2) == 1
    even = lax.rem(s, 2) == 0

    def copy(src, dst, send, recv, section):
        return pltpu.make_async_remote_copy(
            src_ref=src,
            dst_ref=dst,
            send_sem=send,
            recv_sem=recv,
            device_id={"section": section},
            device_id_type=MESH,
        )

    def group_cols(g):
        return pl.ds(pl.multiple_of(g * width, HS), width)

    def head_cols(h):
        return pl.ds(pl.multiple_of(h * HS, HS), HS)

    near = [(-1, s >= 1), (-2, s >= 2), (1, s + 1 < n), (2, s + 2 < n)]

    barrier = pltpu.get_barrier_semaphore()
    for step, there in near:
        @pl.when(there)
        def _():
            pl.semaphore_signal(
                barrier, inc=1, device_id={"section": s + step}, device_id_type=MESH
            )
    for j in range(1, tp):
        pl.semaphore_signal(
            barrier, inc=1, device_id={"tp": lax.rem(t + j, tp)}, device_id_type=MESH
        )
    pl.semaphore_wait(barrier, jnp.minimum(s, 2) + jnp.minimum(n - 1 - s, 2) + tp - 1)

    doc_own[...] = jnp.broadcast_to(doc_ref[...], doc_own.shape)
    back = [2, 3, 0, 1]

    def doc_copy(i):
        return copy(
            doc_own, doc_buf.at[back[i]], doc_send.at[i], doc_recv.at[back[i]], s + near[i][0]
        )

    for i in range(4):
        @pl.when(near[i][1])
        def _():
            doc_copy(i).start()

    kv_src = (k_ref, v_ref)
    qo_src = (q_ref, do_ref)

    def kv_copy(a, slot, g, src, section):
        c = group_cols(g)
        return copy(
            src.at[:, c], kv_buf.at[a, slot, :, c], kv_send.at[a, slot, g],
            kv_recv.at[a, slot, g], section,
        )

    def qo_copy(a, slot, g, src, section):
        c = group_cols(g)
        return copy(
            src.at[:, c], qo_buf.at[a, slot, :, c], qo_send.at[a, slot, g],
            qo_recv.at[a, slot, g], section,
        )

    def kv_start(g):
        for a in range(2):
            @pl.when(even)
            def _():
                kv_copy(a, 0, g, kv_src[a], s + 1).start()

            @pl.when(s + 2 < n)
            def _():
                kv_copy(a, 1, g, kv_src[a], s + 2).start()

    def qo_start(a, g):
        @pl.when(odd)
        def _():
            qo_copy(a, 0, g, qo_src[a], s - 1).start()

        @pl.when(s >= 2)
        def _():
            qo_copy(a, 1, g, qo_src[a], s - 2).start()

    def kv_arrive(g):
        @pl.when(s >= 2)
        def _():
            for a in range(2):
                kv_copy(a, 1, g, kv_src[a], s).wait_recv()

                @pl.when(odd)
                def _():
                    kv_copy(a, 0, g, kv_buf.at[a, 1], s - 1).start()

        @pl.when(s >= 1)
        def _():
            for a in range(2):
                kv_copy(a, 0, g, kv_src[a], s).wait_recv()

    def qo_far_arrive(a, g):
        @pl.when((s + 2 < n) & (g >= 0) & (g < GROUPS))
        def _():
            qo_copy(a, 1, g, qo_src[a], s).wait_recv()

            @pl.when(even)
            def _():
                qo_copy(a, 0, g, qo_buf.at[a, 1], s + 1).start()

    def qo_near_arrive(g):
        @pl.when(s + 1 < n)
        def _():
            for a in range(2):
                qo_copy(a, 0, g, qo_src[a], s).wait_recv()

    def loop(count, f):
        lax.fori_loop(0, count, lambda i, c: (f(i), c)[1], 0)

    loop(GROUPS, kv_start)

    for slot in range(2):
        @pl.when(s < slot + 1)
        def _():
            kv_buf[:, slot] = jnp.zeros((2, rows, cols), kv_buf.dtype)
            doc_buf[slot] = jnp.zeros(doc_buf.shape[1:], doc_buf.dtype)

        @pl.when(s + slot + 1 >= n)
        def _():
            qo_buf[:, slot] = jnp.zeros((2, rows, cols), qo_buf.dtype)
            stat_buf[slot] = jnp.zeros(stat_buf.shape[1:], stat_buf.dtype)
            doc_buf[2 + slot] = jnp.zeros(doc_buf.shape[1:], doc_buf.dtype)

    sums[...] = jnp.zeros(sums.shape, sums.dtype)
    stat_col[...] = jnp.zeros(stat_col.shape, stat_col.dtype)

    doc_row = doc_ref[...].astype(jnp.float32)
    doc_col = jnp.transpose(jnp.broadcast_to(doc_row, (HS, rows)))[:, :1]
    for i in range(4):
        @pl.when(near[i][1])
        def _():
            doc_copy(i).wait_send()
            copy(doc_own, doc_buf.at[i], doc_send.at[i], doc_recv.at[i], s).wait_recv()
    down = lax.broadcasted_iota(jnp.int32, (rows, rows), 0)
    across = lax.broadcasted_iota(jnp.int32, (rows, rows), 1)

    spans = (slice(0, rows), slice(rows, 3 * rows))

    def bias(visible):
        return jnp.where(visible, 0.0, HIDDEN)

    same = doc_col == doc_row
    bias_ref[:, spans[0]] = bias(same & (down >= across))
    bias_t_ref[:, spans[0]] = bias(same & (across >= down))
    for i in range(2):
        for ref, slot, where_far in ((bias_ref, i, down < across), (bias_t_ref, i + 2, across < down)):
            other = doc_buf[slot][:1].astype(jnp.float32)
            visible = (doc_col == other) & near[slot][1]
            if i == 1:
                visible = visible & where_far
            ref[:, (i + 1) * rows : (i + 2) * rows] = bias(visible)

    lane = lax.broadcasted_iota(jnp.int32, (rows, HS), 1)

    def keys_of(j, c):
        return k_ref[:, c] if j == 0 else kv_buf[0, :, :, c].reshape(2 * rows, HS)

    def values_of(j, c):
        return v_ref[:, c] if j == 0 else kv_buf[1, :, :, c].reshape(2 * rows, HS)

    def forward_head(h):
        c = head_cols(h)
        q = q_ref[:, c]
        scores = [nt_dot(q, keys_of(j, c)) * scale2 + bias_ref[:, spans[j]] for j in range(2)]
        top = jnp.maximum(
            jnp.max(scores[0], axis=-1, keepdims=True), jnp.max(scores[1], axis=-1, keepdims=True)
        )
        parts = [jnp.exp2(x - top) for x in scores]
        total = jnp.sum(parts[0], axis=-1, keepdims=True) + jnp.sum(
            parts[1], axis=-1, keepdims=True
        )
        recip = 1.0 / total
        att = jnp.zeros((rows, HS), jnp.float32)
        for j in range(2):
            w = (parts[j] * recip).astype(jnp.bfloat16)
            w_ref[h, :, spans[j]] = w
            att = att + nn_dot(w, values_of(j, c))
        att_ref[:, c] = att
        stat_col[0] = jnp.where(lane == h, top + jnp.log2(total), stat_col[0])
        sums[0] += att * att
        sums[1] += cot_ref[:, c].astype(jnp.float32) * gain_ref[:, c] * att

    def forward_group(g):
        kv_arrive(g)

        @pl.when(g == GROUPS - 1)
        def _():
            loop(GROUPS, lambda i: qo_start(0, i))

        loop(per_group, lambda i: forward_head(g * per_group + i))

    loop(GROUPS, forward_group)

    def sums_copy(j):
        return pltpu.make_async_remote_copy(
            src_ref=sums,
            dst_ref=sums_buf.at[j - 1],
            send_sem=sums_send.at[j - 1],
            recv_sem=sums_recv.at[j - 1],
            device_id={"tp": lax.rem(t + j, tp)},
            device_id_type=MESH,
        )

    for j in range(1, tp):
        sums_copy(j).start()
    for g in range(2):
        qo_far_arrive(0, g)
    squares, inner = sums[0], sums[1]
    for j in range(1, tp):
        sums_copy(j).wait()
        squares = squares + sums_buf[j - 1, 0]
        inner = inner + sums_buf[j - 1, 1]
    inverse = lax.rsqrt(jnp.sum(squares, axis=-1, keepdims=True) / features + 1e-05)
    factor = inverse * inverse * inverse * jnp.sum(inner, axis=-1, keepdims=True) / features
    sums[0] = jnp.broadcast_to(inverse, (rows, HS))
    sums[1] = jnp.broadcast_to(factor, (rows, HS))

    def norm_head(h):
        c = head_cols(h)
        att = att_ref[:, c]
        gain = gain_ref[:, c]
        normed_ref[:, c] = (att * sums[0] * gain).astype(normed_ref.dtype)
        grad = sums[0] * (cot_ref[:, c].astype(jnp.float32) * gain) - att * sums[1]
        grad = grad.astype(do_ref.dtype)
        do_ref[:, c] = grad
        delta = jnp.sum(grad.astype(jnp.float32) * att, axis=-1, keepdims=True)
        stat_col[1] = jnp.where(lane == h, delta, stat_col[1])

    def norm_group(g):
        loop(per_group, lambda i: norm_head(g * per_group + i))
        qo_start(1, g)

    loop(GROUPS, norm_group)
    for i in range(2):
        stat_own[i] = jnp.transpose(stat_col[i])[:hp]

    def stat_copy(slot):
        return copy(
            stat_own, stat_buf.at[slot], stat_send.at[slot], stat_recv.at[slot], s - slot - 1
        )

    for slot in range(2):
        @pl.when(s >= slot + 1)
        def _():
            stat_copy(slot).start()
    def query_head(h):
        c = head_cols(h)
        grad = do_ref[:, c]
        delta = jnp.sum(grad.astype(jnp.float32) * att_ref[:, c], axis=-1, keepdims=True)
        dq = jnp.zeros((rows, HS), jnp.float32)
        for j in range(2):
            w = w_ref[h, :, spans[j]].astype(jnp.float32)
            ds = (w * (nt_dot(grad, values_of(j, c)) - delta)).astype(jnp.bfloat16)
            dq = dq + nn_dot(ds, keys_of(j, c))
        dq_ref[:, c] = (dq * scale).astype(dq_ref.dtype)

    def key_terms(h, q, grad, mask, log_total, delta):
        c = head_cols(h)
        w = jnp.exp2(nt_dot(k_ref[:, c], q) * scale2 + mask - log_total)
        ds = (w * (nt_dot(v_ref[:, c], grad) - delta)).astype(jnp.bfloat16)
        return nn_dot(ds, q), nn_dot(w.astype(jnp.bfloat16), grad)

    def local_head(h):
        c = head_cols(h)
        query_head(h)
        log_total, delta = [stat_own[i, pl.ds(h, 1), :] for i in range(2)]
        dk, dv = key_terms(h, q_ref[:, c], do_ref[:, c], bias_t_ref[:, spans[0]], log_total, delta)
        dk_acc[:, c] = dk
        dv_acc[:, c] = dv

    def remote_head(h):
        c = head_cols(h)
        q, grad = [qo_buf[a, :, :, c].reshape(2 * rows, HS) for a in range(2)]
        log_total, delta = [
            jnp.concatenate([stat_buf[j, i, pl.ds(h, 1), :] for j in range(2)], axis=1)
            for i in range(2)
        ]
        dk, dv = key_terms(h, q, grad, bias_t_ref[:, spans[1]], log_total, delta)
        dk_ref[:, c] = ((dk_acc[:, c] + dk) * scale).astype(dk_ref.dtype)
        dv_ref[:, c] = (dv_acc[:, c] + dv).astype(dv_ref.dtype)

    def local_group(g):
        loop(per_group, lambda i: local_head(g * per_group + i))
        qo_far_arrive(0, g + 2)
        qo_far_arrive(1, g - 2)

    loop(GROUPS, local_group)

    for slot in range(2):
        @pl.when(s + slot + 1 < n)
        def _():
            copy(
                stat_own, stat_buf.at[slot], stat_send.at[slot], stat_recv.at[slot], s
            ).wait_recv()


    def remote_group(g):
        qo_far_arrive(1, g + GROUPS - 2)
        qo_near_arrive(g)
        loop(per_group, lambda i: remote_head(g * per_group + i))

    loop(GROUPS, remote_group)

    for slot in range(2):
        @pl.when(s >= slot + 1)
        def _():
            stat_copy(slot).wait_send()

    def sent(g):
        for a in range(2):
            @pl.when(even | (s >= 3))
            def _():
                kv_copy(a, 0, g, kv_src[a], s).wait_send()

            @pl.when(s + 2 < n)
            def _():
                kv_copy(a, 1, g, kv_src[a], s).wait_send()

            @pl.when(odd | (s + 3 < n))
            def _():
                qo_copy(a, 0, g, qo_src[a], s).wait_send()

            @pl.when(s >= 2)
            def _():
                qo_copy(a, 1, g, qo_src[a], s).wait_send()

    loop(GROUPS, sent)


def body(n, tp, queries, keys, values, cotangent, doc_ids, gain):
    rows, cols = queries.shape
    heads = cols // HS
    hp = -(-heads // 8) * 8
    vmem = pl.BlockSpec(memory_space=pltpu.VMEM)
    bf16, f32 = jnp.bfloat16, jnp.float32
    dma = pltpu.SemaphoreType.DMA
    out = jax.ShapeDtypeStruct((rows, cols), bf16)
    return pl.pallas_call(
        functools.partial(kernel, n, tp),
        out_shape=(out,) * 4,
        in_specs=[vmem] * 6,
        out_specs=(vmem,) * 4,
        scratch_shapes=[
            pltpu.VMEM((2, 2, rows, cols), bf16),
            pltpu.VMEM((2, 2, rows, cols), bf16),
            pltpu.VMEM((rows, cols), bf16),
            pltpu.VMEM((rows, cols), f32),
            pltpu.VMEM((heads, rows, 3 * rows), bf16),
            pltpu.VMEM((rows, 3 * rows), f32),
            pltpu.VMEM((rows, 3 * rows), f32),
            pltpu.VMEM((rows, cols), f32),
            pltpu.VMEM((rows, cols), f32),
            pltpu.VMEM((8, rows), jnp.int32),
            pltpu.VMEM((4, 8, rows), jnp.int32),
            pltpu.VMEM((2, rows, HS), f32),
            pltpu.VMEM((max(tp - 1, 1), 2, rows, HS), f32),
            pltpu.VMEM((2, rows, HS), f32),
            pltpu.VMEM((2, hp, rows), f32),
            pltpu.VMEM((2, 2, hp, rows), f32),
            dma((2, 2, GROUPS)),
            dma((2, 2, GROUPS)),
            dma((2, 2, GROUPS)),
            dma((2, 2, GROUPS)),
            dma((4,)),
            dma((4,)),
            dma((max(tp - 1, 1),)),
            dma((max(tp - 1, 1),)),
            dma((2,)),
            dma((2,)),
        ],
        compiler_params=pltpu.CompilerParams(
            collective_id=0, has_side_effects=True, vmem_limit_bytes=60 * 1024 * 1024
        ),
        cost_estimate=pl.CostEstimate(
            flops=16 * heads * 3 * rows * rows * HS,
            bytes_accessed=16 * rows * cols,
            transcendentals=6 * heads * rows * rows,
        ),
    )(queries, keys, values, cotangent, doc_ids.reshape(1, rows), gain.reshape(1, cols))


def solution(mesh):
    wide = P("section", "tp")
    return jax.shard_map(
        functools.partial(body, mesh.shape["section"], mesh.shape["tp"]),
        mesh=mesh,
        in_specs=(wide, wide, wide, wide, P("section"), P("tp")),
        out_specs=(wide,) * 4,
        check_vma=False,
    )
```

```python
import functools
import math

import jax
import jax.numpy as jnp
from jax import lax
from jax.experimental import pallas as pl
from jax.experimental.pallas import tpu as pltpu
from jax.sharding import PartitionSpec as P

HS = 128
GROUPS = 6
AHEAD = 3
MESH = pl.DeviceIdType.MESH
LOG2E = math.log2(math.e)
HIDDEN = -1e30
NT = (((1,), (1,)), ((), ()))


def nt_dot(a, b):
    return lax.dot_general(a, b, NT, preferred_element_type=jnp.float32)


def nn_dot(a, b):
    return jnp.dot(a, b, preferred_element_type=jnp.float32)


def kernel(
    n,
    tp,
    q_ref,
    k_ref,
    v_ref,
    cot_ref,
    doc_ref,
    gain_ref,
    normed_ref,
    dq_ref,
    dk_ref,
    dv_ref,
    kv_buf,
    qo_buf,
    do_ref,
    att_ref,
    w_ref,
    bias_ref,
    bias_t_ref,
    dk_acc,
    dv_acc,
    doc_own,
    doc_buf,
    sums,
    sums_buf,
    stat_col,
    stat_own,
    stat_buf,
    kv_send,
    kv_recv,
    qo_send,
    qo_recv,
    doc_send,
    doc_recv,
    sums_send,
    sums_recv,
    stat_send,
    stat_recv,
):
    rows, cols = q_ref.shape
    heads = cols // HS
    per_group = heads // GROUPS
    width = per_group * HS
    features = cols * tp
    scale = HS ** (-0.5)
    scale2 = scale * LOG2E
    hp = stat_own.shape[1]
    s = lax.axis_index("section")
    t = lax.axis_index("tp")
    odd = lax.rem(s, 2) == 1
    even = lax.rem(s, 2) == 0

    def copy(src, dst, send, recv, section):
        return pltpu.make_async_remote_copy(
            src_ref=src,
            dst_ref=dst,
            send_sem=send,
            recv_sem=recv,
            device_id={"section": section},
            device_id_type=MESH,
        )

    def group_cols(g):
        return pl.ds(pl.multiple_of(g * width, HS), width)

    def head_cols(h):
        return pl.ds(pl.multiple_of(h * HS, HS), HS)

    near = [(-1, s >= 1), (-2, s >= 2), (1, s + 1 < n), (2, s + 2 < n)]

    barrier = pltpu.get_barrier_semaphore()
    for step, there in near:
        @pl.when(there)
        def _():
            pl.semaphore_signal(
                barrier, inc=1, device_id={"section": s + step}, device_id_type=MESH
            )
    for j in range(1, tp):
        pl.semaphore_signal(
            barrier, inc=1, device_id={"tp": lax.rem(t + j, tp)}, device_id_type=MESH
        )
    pl.semaphore_wait(barrier, jnp.minimum(s, 2) + jnp.minimum(n - 1 - s, 2) + tp - 1)

    doc_own[...] = jnp.broadcast_to(doc_ref[...], doc_own.shape)
    back = [2, 3, 0, 1]

    def doc_copy(i):
        return copy(
            doc_own, doc_buf.at[back[i]], doc_send.at[i], doc_recv.at[back[i]], s + near[i][0]
        )

    for i in range(4):
        @pl.when(near[i][1])
        def _():
            doc_copy(i).start()

    kv_src = (k_ref, v_ref)
    qo_src = (q_ref, do_ref)

    def kv_copy(a, slot, g, src, section):
        c = group_cols(g)
        return copy(
            src.at[:, c], kv_buf.at[a, slot, :, c], kv_send.at[a, slot, g],
            kv_recv.at[a, slot, g], section,
        )

    def qo_copy(a, slot, g, src, section):
        c = group_cols(g)
        return copy(
            src.at[:, c], qo_buf.at[a, slot, :, c], qo_send.at[a, slot, g],
            qo_recv.at[a, slot, g], section,
        )

    first = lax.rem(t, 2) == 0
    second = lax.rem(t, 2) == 1

    def in_turn(one, other):
        pl.when(one[0] & first)(lambda: one[1]())
        pl.when(other[0])(lambda: other[1]())
        pl.when(one[0] & second)(lambda: one[1]())

    def kv_start(a, g):
        in_turn(
            (even, lambda: kv_copy(a, 0, g, kv_src[a], s + 1).start()),
            (s + 2 < n, lambda: kv_copy(a, 1, g, kv_src[a], s + 2).start()),
        )

    def kv_arrive(a, g):
        @pl.when(s >= 2)
        def _():
            kv_copy(a, 1, g, kv_src[a], s).wait_recv()

        more = odd & (s + 2 < n) & (g + 1 < GROUPS)
        in_turn(
            (odd & (s >= 3), lambda: kv_copy(a, 0, g, kv_buf.at[a, 1], s - 1).start()),
            (more, lambda: kv_copy(a, 1, g + 1, kv_src[a], s + 2).start()),
        )

    def kv_near_arrive(a, g):
        @pl.when(s >= 1)
        def _():
            kv_copy(a, 0, g, kv_src[a], s).wait_recv()

    def stream(i, f):
        for a in range(2):
            pl.when((i >= a * GROUPS) & (i < (a + 1) * GROUPS))(lambda: f(a, i - a * GROUPS))

    def qo_start(i):
        def start(a, g):
            in_turn(
                (odd, lambda: qo_copy(a, 0, g, qo_src[a], s - 1).start()),
                (s >= 2, lambda: qo_copy(a, 1, g, qo_src[a], s - 2).start()),
            )

        stream(i, start)

    def qo_pass(k):
        passes = even & (s + 2 < n)

        @pl.when(s + 2 < n)
        def _():
            stream(k, lambda a, g: qo_copy(a, 1, g, qo_src[a], s).wait_recv())

        in_turn(
            (
                passes,
                lambda: stream(
                    k, lambda a, g: qo_copy(a, 0, g, qo_buf.at[a, 1], s + 1).start()
                ),
            ),
            (k + AHEAD >= 0, lambda: qo_start(k + AHEAD)),
        )

    def qo_near_arrive(g):
        @pl.when(s + 1 < n)
        def _():
            for a in range(2):
                qo_copy(a, 0, g, qo_src[a], s).wait_recv()

    def loop(count, f):
        lax.fori_loop(0, count, lambda i, c: (f(i), c)[1], 0)

    def kv_first(g):
        @pl.when(even | (g == 0))
        def _():
            for a in range(2):
                kv_start(a, g)

    loop(GROUPS, kv_first)

    for slot in range(2):
        @pl.when(s < slot + 1)
        def _():
            kv_buf[:, slot] = jnp.zeros((2, rows, cols), kv_buf.dtype)
            doc_buf[slot] = jnp.zeros(doc_buf.shape[1:], doc_buf.dtype)

        @pl.when(s + slot + 1 >= n)
        def _():
            qo_buf[:, slot] = jnp.zeros((2, rows, cols), qo_buf.dtype)
            stat_buf[slot] = jnp.zeros(stat_buf.shape[1:], stat_buf.dtype)
            doc_buf[2 + slot] = jnp.zeros(doc_buf.shape[1:], doc_buf.dtype)

    sums[...] = jnp.zeros(sums.shape, sums.dtype)
    stat_col[...] = jnp.zeros(stat_col.shape, stat_col.dtype)

    doc_row = doc_ref[...].astype(jnp.float32)
    doc_col = jnp.transpose(jnp.broadcast_to(doc_row, (HS, rows)))[:, :1]
    for i in range(4):
        @pl.when(near[i][1])
        def _():
            doc_copy(i).wait_send()
            copy(doc_own, doc_buf.at[i], doc_send.at[i], doc_recv.at[i], s).wait_recv()
    down = lax.broadcasted_iota(jnp.int32, (rows, rows), 0)
    across = lax.broadcasted_iota(jnp.int32, (rows, rows), 1)

    spans = (slice(0, rows), slice(rows, 3 * rows))

    def bias(visible):
        return jnp.where(visible, 0.0, HIDDEN)

    same = doc_col == doc_row
    bias_ref[:, spans[0]] = bias(same & (down >= across))
    bias_t_ref[:, spans[0]] = bias(same & (across >= down))
    for i in range(2):
        for ref, slot, where_far in ((bias_ref, i, down < across), (bias_t_ref, i + 2, across < down)):
            other = doc_buf[slot][:1].astype(jnp.float32)
            visible = (doc_col == other) & near[slot][1]
            if i == 1:
                visible = visible & where_far
            ref[:, (i + 1) * rows : (i + 2) * rows] = bias(visible)

    lane = lax.broadcasted_iota(jnp.int32, (rows, HS), 1)

    def keys_of(j, c):
        return k_ref[:, c] if j == 0 else kv_buf[0, :, :, c].reshape(2 * rows, HS)

    def values_of(j, c):
        return v_ref[:, c] if j == 0 else kv_buf[1, :, :, c].reshape(2 * rows, HS)

    def forward_head(h):
        c = head_cols(h)
        q = q_ref[:, c]
        scores = [nt_dot(q, keys_of(j, c)) * scale2 + bias_ref[:, spans[j]] for j in range(2)]
        top = jnp.maximum(
            jnp.max(scores[0], axis=-1, keepdims=True), jnp.max(scores[1], axis=-1, keepdims=True)
        )
        parts = [jnp.exp2(x - top) for x in scores]
        total = jnp.sum(parts[0], axis=-1, keepdims=True) + jnp.sum(
            parts[1], axis=-1, keepdims=True
        )
        recip = 1.0 / total
        att = jnp.zeros((rows, HS), jnp.float32)
        for j in range(2):
            w = (parts[j] * recip).astype(jnp.bfloat16)
            w_ref[h, :, spans[j]] = w
            att = att + nn_dot(w, values_of(j, c))
        att_ref[:, c] = att
        stat_col[0] = jnp.where(lane == h, top + jnp.log2(total), stat_col[0])
        sums[0] += att * att
        sums[1] += cot_ref[:, c].astype(jnp.float32) * gain_ref[:, c] * att

    def forward_group(g):
        for a in range(2):
            kv_arrive(a, g)
        for a in range(2):
            kv_near_arrive(a, g)

        @pl.when(g == GROUPS - 1)
        def _():
            qo_start(0)

        loop(per_group, lambda i: forward_head(g * per_group + i))

    loop(GROUPS, forward_group)

    def sums_copy(j):
        return pltpu.make_async_remote_copy(
            src_ref=sums,
            dst_ref=sums_buf.at[j - 1],
            send_sem=sums_send.at[j - 1],
            recv_sem=sums_recv.at[j - 1],
            device_id={"tp": lax.rem(t + j, tp)},
            device_id_type=MESH,
        )

    for j in range(1, tp):
        sums_copy(j).start()
    for i in range(1, AHEAD):
        qo_start(i)
    squares, inner = sums[0], sums[1]
    for j in range(1, tp):
        sums_copy(j).wait()
        squares = squares + sums_buf[j - 1, 0]
        inner = inner + sums_buf[j - 1, 1]
    inverse = lax.rsqrt(jnp.sum(squares, axis=-1, keepdims=True) / features + 1e-05)
    factor = inverse * inverse * inverse * jnp.sum(inner, axis=-1, keepdims=True) / features
    sums[0] = jnp.broadcast_to(inverse, (rows, HS))
    sums[1] = jnp.broadcast_to(factor, (rows, HS))

    def norm_head(h):
        c = head_cols(h)
        att = att_ref[:, c]
        gain = gain_ref[:, c]
        normed_ref[:, c] = (att * sums[0] * gain).astype(normed_ref.dtype)
        grad = sums[0] * (cot_ref[:, c].astype(jnp.float32) * gain) - att * sums[1]
        grad = grad.astype(do_ref.dtype)
        do_ref[:, c] = grad
        delta = jnp.sum(grad.astype(jnp.float32) * att, axis=-1, keepdims=True)
        stat_col[1] = jnp.where(lane == h, delta, stat_col[1])

    def norm_group(g):
        loop(per_group, lambda i: norm_head(g * per_group + i))

    loop(GROUPS, norm_group)
    for i in range(2):
        stat_own[i] = jnp.transpose(stat_col[i])[:hp]

    def stat_copy(slot):
        return copy(
            stat_own, stat_buf.at[slot], stat_send.at[slot], stat_recv.at[slot], s - slot - 1
        )

    for slot in range(2):
        @pl.when(s >= slot + 1)
        def _():
            stat_copy(slot).start()
    def query_head(h):
        c = head_cols(h)
        grad = do_ref[:, c]
        delta = jnp.sum(grad.astype(jnp.float32) * att_ref[:, c], axis=-1, keepdims=True)
        dq = jnp.zeros((rows, HS), jnp.float32)
        for j in range(2):
            w = w_ref[h, :, spans[j]].astype(jnp.float32)
            ds = (w * (nt_dot(grad, values_of(j, c)) - delta)).astype(jnp.bfloat16)
            dq = dq + nn_dot(ds, keys_of(j, c))
        dq_ref[:, c] = (dq * scale).astype(dq_ref.dtype)

    def key_terms(h, q, grad, mask, log_total, delta):
        c = head_cols(h)
        w = jnp.exp2(nt_dot(k_ref[:, c], q) * scale2 + mask - log_total)
        ds = (w * (nt_dot(v_ref[:, c], grad) - delta)).astype(jnp.bfloat16)
        return nn_dot(ds, q), nn_dot(w.astype(jnp.bfloat16), grad)

    def local_head(h):
        c = head_cols(h)
        query_head(h)
        log_total, delta = [stat_own[i, pl.ds(h, 1), :] for i in range(2)]
        dk, dv = key_terms(h, q_ref[:, c], do_ref[:, c], bias_t_ref[:, spans[0]], log_total, delta)
        dk_acc[:, c] = dk
        dv_acc[:, c] = dv

    def remote_head(h):
        c = head_cols(h)
        q, grad = [qo_buf[a, :, :, c].reshape(2 * rows, HS) for a in range(2)]
        log_total, delta = [
            jnp.concatenate([stat_buf[j, i, pl.ds(h, 1), :] for j in range(2)], axis=1)
            for i in range(2)
        ]
        dk, dv = key_terms(h, q, grad, bias_t_ref[:, spans[1]], log_total, delta)
        dk_ref[:, c] = ((dk_acc[:, c] + dk) * scale).astype(dk_ref.dtype)
        dv_ref[:, c] = (dv_acc[:, c] + dv).astype(dv_ref.dtype)

    for k in range(2):
        qo_pass(k)

    def local_group(g):
        for i in range(per_group):
            local_head(g * per_group + i)
            if i < 2:
                qo_pass(2 * g + 2 + i)

    half = GROUPS // 2
    loop(half, local_group)

    for slot in range(2):
        @pl.when(s + slot + 1 < n)
        def _():
            copy(
                stat_own, stat_buf.at[slot], stat_send.at[slot], stat_recv.at[slot], s
            ).wait_recv()

    def remote_group(g):
        qo_near_arrive(g)
        loop(per_group, lambda i: remote_head(g * per_group + i))

    def both_groups(i):
        local_group(half + i)
        loop(2, lambda j: remote_group(2 * i + j))

    loop(half, both_groups)

    for slot in range(2):
        @pl.when(s >= slot + 1)
        def _():
            stat_copy(slot).wait_send()

    def sent(g):
        for a in range(2):
            @pl.when(even | (s >= 3))
            def _():
                kv_copy(a, 0, g, kv_src[a], s).wait_send()

            @pl.when(s + 2 < n)
            def _():
                kv_copy(a, 1, g, kv_src[a], s).wait_send()

            @pl.when(odd | (s + 3 < n))
            def _():
                qo_copy(a, 0, g, qo_src[a], s).wait_send()

            @pl.when(s >= 2)
            def _():
                qo_copy(a, 1, g, qo_src[a], s).wait_send()

    loop(GROUPS, sent)


def body(n, tp, queries, keys, values, cotangent, doc_ids, gain):
    rows, cols = queries.shape
    heads = cols // HS
    hp = -(-heads // 8) * 8
    vmem = pl.BlockSpec(memory_space=pltpu.VMEM)
    bf16, f32 = jnp.bfloat16, jnp.float32
    dma = pltpu.SemaphoreType.DMA
    out = jax.ShapeDtypeStruct((rows, cols), bf16)
    return pl.pallas_call(
        functools.partial(kernel, n, tp),
        out_shape=(out,) * 4,
        in_specs=[vmem] * 6,
        out_specs=(vmem,) * 4,
        scratch_shapes=[
            pltpu.VMEM((2, 2, rows, cols), bf16),
            pltpu.VMEM((2, 2, rows, cols), bf16),
            pltpu.VMEM((rows, cols), bf16),
            pltpu.VMEM((rows, cols), f32),
            pltpu.VMEM((heads, rows, 3 * rows), bf16),
            pltpu.VMEM((rows, 3 * rows), f32),
            pltpu.VMEM((rows, 3 * rows), f32),
            pltpu.VMEM((rows, cols), f32),
            pltpu.VMEM((rows, cols), f32),
            pltpu.VMEM((8, rows), jnp.int32),
            pltpu.VMEM((4, 8, rows), jnp.int32),
            pltpu.VMEM((2, rows, HS), f32),
            pltpu.VMEM((max(tp - 1, 1), 2, rows, HS), f32),
            pltpu.VMEM((2, rows, HS), f32),
            pltpu.VMEM((2, hp, rows), f32),
            pltpu.VMEM((2, 2, hp, rows), f32),
            dma((2, 2, GROUPS)),
            dma((2, 2, GROUPS)),
            dma((2, 2, GROUPS)),
            dma((2, 2, GROUPS)),
            dma((4,)),
            dma((4,)),
            dma((max(tp - 1, 1),)),
            dma((max(tp - 1, 1),)),
            dma((2,)),
            dma((2,)),
        ],
        compiler_params=pltpu.CompilerParams(
            collective_id=0, has_side_effects=True, vmem_limit_bytes=60 * 1024 * 1024
        ),
        cost_estimate=pl.CostEstimate(
            flops=16 * heads * 3 * rows * rows * HS,
            bytes_accessed=16 * rows * cols,
            transcendentals=6 * heads * rows * rows,
        ),
    )(queries, keys, values, cotangent, doc_ids.reshape(1, rows), gain.reshape(1, cols))


def solution(mesh):
    wide = P("section", "tp")
    return jax.shard_map(
        functools.partial(body, mesh.shape["section"], mesh.shape["tp"]),
        mesh=mesh,
        in_specs=(wide, wide, wide, wide, P("section"), P("tp")),
        out_specs=(wide,) * 4,
        check_vma=False,
    )
```

```python
import functools
import math

import jax
import jax.numpy as jnp
from jax import lax
from jax.experimental import pallas as pl
from jax.experimental.pallas import tpu as pltpu
from jax.sharding import PartitionSpec as P

HS = 128
GROUPS = 6
DEPTH = 2
AHEAD = 4
MESH = pl.DeviceIdType.MESH
LOG2E = math.log2(math.e)
HIDDEN = -1e30
NT = (((1,), (1,)), ((), ()))


def nt_dot(a, b):
    return lax.dot_general(a, b, NT, preferred_element_type=jnp.float32)


def nn_dot(a, b):
    return jnp.dot(a, b, preferred_element_type=jnp.float32)


def kernel(
    n,
    tp,
    q_ref,
    k_ref,
    v_ref,
    cot_ref,
    doc_ref,
    gain_ref,
    normed_ref,
    dq_ref,
    dk_ref,
    dv_ref,
    kv_buf,
    qo_buf,
    do_ref,
    att_ref,
    w_ref,
    bias_ref,
    bias_t_ref,
    dk_acc,
    dv_acc,
    doc_own,
    doc_buf,
    sums,
    sums_buf,
    stat_col,
    stat_own,
    stat_buf,
    kv_send,
    kv_recv,
    qo_send,
    qo_recv,
    doc_send,
    doc_recv,
    sums_send,
    sums_recv,
    stat_send,
    stat_recv,
):
    rows, cols = q_ref.shape
    heads = cols // HS
    per_group = heads // GROUPS
    width = per_group * HS
    features = cols * tp
    scale = HS ** (-0.5)
    scale2 = scale * LOG2E
    hp = stat_own.shape[1]
    s = lax.axis_index("section")
    t = lax.axis_index("tp")
    odd = lax.rem(s, 2) == 1
    even = lax.rem(s, 2) == 0

    def copy(src, dst, send, recv, section):
        return pltpu.make_async_remote_copy(
            src_ref=src,
            dst_ref=dst,
            send_sem=send,
            recv_sem=recv,
            device_id={"section": section},
            device_id_type=MESH,
        )

    def group_cols(g):
        return pl.ds(pl.multiple_of(g * width, HS), width)

    def head_cols(h):
        return pl.ds(pl.multiple_of(h * HS, HS), HS)

    near = [(-1, s >= 1), (-2, s >= 2), (1, s + 1 < n), (2, s + 2 < n)]

    barrier = pltpu.get_barrier_semaphore()
    for step, there in near:
        @pl.when(there)
        def _():
            pl.semaphore_signal(
                barrier, inc=1, device_id={"section": s + step}, device_id_type=MESH
            )
    for j in range(1, tp):
        pl.semaphore_signal(
            barrier, inc=1, device_id={"tp": lax.rem(t + j, tp)}, device_id_type=MESH
        )
    pl.semaphore_wait(barrier, jnp.minimum(s, 2) + jnp.minimum(n - 1 - s, 2) + tp - 1)

    doc_own[...] = jnp.broadcast_to(doc_ref[...], doc_own.shape)
    back = [2, 3, 0, 1]

    def doc_copy(i):
        return copy(
            doc_own, doc_buf.at[back[i]], doc_send.at[i], doc_recv.at[back[i]], s + near[i][0]
        )

    for i in range(4):
        @pl.when(near[i][1])
        def _():
            doc_copy(i).start()

    kv_src = (k_ref, v_ref)
    qo_src = (q_ref, do_ref)

    def kv_copy(a, slot, g, src, section):
        c = group_cols(g)
        return copy(
            src.at[:, c], kv_buf.at[a, slot, :, c], kv_send.at[a, slot, g],
            kv_recv.at[a, slot, g], section,
        )

    def qo_copy(a, slot, g, src, section):
        c = group_cols(g)
        return copy(
            src.at[:, c], qo_buf.at[a, slot, :, c], qo_send.at[a, slot, g],
            qo_recv.at[a, slot, g], section,
        )

    first = lax.rem(t, 2) == 0
    second = lax.rem(t, 2) == 1

    def in_turn(one, other):
        pl.when(one[0] & first)(lambda: one[1]())
        pl.when(other[0])(lambda: other[1]())
        pl.when(one[0] & second)(lambda: one[1]())

    def kv_start(a, g):
        in_turn(
            (even, lambda: kv_copy(a, 0, g, kv_src[a], s + 1).start()),
            (s + 2 < n, lambda: kv_copy(a, 1, g, kv_src[a], s + 2).start()),
        )

    def kv_pass(a, g):
        @pl.when(s >= 2)
        def _():
            kv_copy(a, 1, g, kv_src[a], s).wait_recv()

            @pl.when(odd)
            def _():
                kv_copy(a, 0, g, kv_buf.at[a, 1], s - 1).start()

    def kv_next(a, g):
        @pl.when(even)
        def _():
            kv_copy(a, 0, g, kv_src[a], s).wait_send()

        @pl.when(s + 2 < n)
        def _():
            kv_copy(a, 1, g, kv_src[a], s).wait_send()

        @pl.when(g + DEPTH < GROUPS)
        def _():
            kv_start(a, g + DEPTH)

    def kv_near_arrive(a, g):
        @pl.when(s >= 1)
        def _():
            kv_copy(a, 0, g, kv_src[a], s).wait_recv()

    def stream(i, f):
        for a in range(2):
            pl.when((i >= a * GROUPS) & (i < (a + 1) * GROUPS))(lambda: f(a, i - a * GROUPS))

    def qo_start(i):
        def start(a, g):
            in_turn(
                (odd, lambda: qo_copy(a, 0, g, qo_src[a], s - 1).start()),
                (s >= 2, lambda: qo_copy(a, 1, g, qo_src[a], s - 2).start()),
            )

        stream(i, start)

    def qo_pass(k):
        passes = even & (s + 2 < n)

        @pl.when(s + 2 < n)
        def _():
            stream(k, lambda a, g: qo_copy(a, 1, g, qo_src[a], s).wait_recv())

        pl.when(passes)(
            lambda: stream(k, lambda a, g: qo_copy(a, 0, g, qo_buf.at[a, 1], s + 1).start())
        )

        @pl.when(odd)
        def _():
            stream(k, lambda a, g: qo_copy(a, 0, g, qo_src[a], s).wait_send())

        @pl.when(s >= 2)
        def _():
            stream(k, lambda a, g: qo_copy(a, 1, g, qo_src[a], s).wait_send())

        qo_start(k + AHEAD)

    def qo_near_arrive(g):
        @pl.when(s + 1 < n)
        def _():
            for a in range(2):
                qo_copy(a, 0, g, qo_src[a], s).wait_recv()

    def loop(count, f):
        lax.fori_loop(0, count, lambda i, c: (f(i), c)[1], 0)

    for g in range(DEPTH):
        for a in range(2):
            kv_start(a, g)

    for slot in range(2):
        @pl.when(s < slot + 1)
        def _():
            kv_buf[:, slot] = jnp.zeros((2, rows, cols), kv_buf.dtype)
            doc_buf[slot] = jnp.zeros(doc_buf.shape[1:], doc_buf.dtype)

        @pl.when(s + slot + 1 >= n)
        def _():
            qo_buf[:, slot] = jnp.zeros((2, rows, cols), qo_buf.dtype)
            stat_buf[slot] = jnp.zeros(stat_buf.shape[1:], stat_buf.dtype)
            doc_buf[2 + slot] = jnp.zeros(doc_buf.shape[1:], doc_buf.dtype)

    sums[...] = jnp.zeros(sums.shape, sums.dtype)
    stat_col[...] = jnp.zeros(stat_col.shape, stat_col.dtype)

    doc_row = doc_ref[...].astype(jnp.float32)
    doc_col = jnp.transpose(jnp.broadcast_to(doc_row, (HS, rows)))[:, :1]
    for i in range(4):
        @pl.when(near[i][1])
        def _():
            doc_copy(i).wait_send()
            copy(doc_own, doc_buf.at[i], doc_send.at[i], doc_recv.at[i], s).wait_recv()
    down = lax.broadcasted_iota(jnp.int32, (rows, rows), 0)
    across = lax.broadcasted_iota(jnp.int32, (rows, rows), 1)

    spans = (slice(0, rows), slice(rows, 3 * rows))

    def bias(visible):
        return jnp.where(visible, 0.0, HIDDEN)

    same = doc_col == doc_row
    bias_ref[:, spans[0]] = bias(same & (down >= across))
    bias_t_ref[:, spans[0]] = bias(same & (across >= down))
    for i in range(2):
        for ref, slot, where_far in ((bias_ref, i, down < across), (bias_t_ref, i + 2, across < down)):
            other = doc_buf[slot][:1].astype(jnp.float32)
            visible = (doc_col == other) & near[slot][1]
            if i == 1:
                visible = visible & where_far
            ref[:, (i + 1) * rows : (i + 2) * rows] = bias(visible)

    lane = lax.broadcasted_iota(jnp.int32, (rows, HS), 1)

    def keys_of(j, c):
        return k_ref[:, c] if j == 0 else kv_buf[0, :, :, c].reshape(2 * rows, HS)

    def values_of(j, c):
        return v_ref[:, c] if j == 0 else kv_buf[1, :, :, c].reshape(2 * rows, HS)

    def forward_head(h):
        c = head_cols(h)
        q = q_ref[:, c]
        scores = [nt_dot(q, keys_of(j, c)) * scale2 + bias_ref[:, spans[j]] for j in range(2)]
        top = jnp.maximum(
            jnp.max(scores[0], axis=-1, keepdims=True), jnp.max(scores[1], axis=-1, keepdims=True)
        )
        parts = [jnp.exp2(x - top) for x in scores]
        total = jnp.sum(parts[0], axis=-1, keepdims=True) + jnp.sum(
            parts[1], axis=-1, keepdims=True
        )
        recip = 1.0 / total
        att = jnp.zeros((rows, HS), jnp.float32)
        for j in range(2):
            w = (parts[j] * recip).astype(jnp.bfloat16)
            w_ref[h, :, spans[j]] = w
            att = att + nn_dot(w, values_of(j, c))
        att_ref[:, c] = att
        stat_col[0] = jnp.where(lane == h, top + jnp.log2(total), stat_col[0])
        sums[0] += att * att
        sums[1] += cot_ref[:, c].astype(jnp.float32) * gain_ref[:, c] * att

    def forward_group(g):
        for a in range(2):
            kv_pass(a, g)
        for a in range(2):
            kv_next(a, g)
        for a in range(2):
            kv_near_arrive(a, g)

        @pl.when(g == GROUPS - 1)
        def _():
            for k in range(AHEAD):
                qo_start(k)

        loop(per_group, lambda i: forward_head(g * per_group + i))

    loop(GROUPS, forward_group)

    def sums_copy(j):
        return pltpu.make_async_remote_copy(
            src_ref=sums,
            dst_ref=sums_buf.at[j - 1],
            send_sem=sums_send.at[j - 1],
            recv_sem=sums_recv.at[j - 1],
            device_id={"tp": lax.rem(t + j, tp)},
            device_id_type=MESH,
        )

    for j in range(1, tp):
        sums_copy(j).start()
    squares, inner = sums[0], sums[1]
    for j in range(1, tp):
        sums_copy(j).wait()
        squares = squares + sums_buf[j - 1, 0]
        inner = inner + sums_buf[j - 1, 1]
    inverse = lax.rsqrt(jnp.sum(squares, axis=-1, keepdims=True) / features + 1e-05)
    factor = inverse * inverse * inverse * jnp.sum(inner, axis=-1, keepdims=True) / features
    sums[0] = jnp.broadcast_to(inverse, (rows, HS))
    sums[1] = jnp.broadcast_to(factor, (rows, HS))

    def norm_head(h):
        c = head_cols(h)
        att = att_ref[:, c]
        gain = gain_ref[:, c]
        normed_ref[:, c] = (att * sums[0] * gain).astype(normed_ref.dtype)
        grad = sums[0] * (cot_ref[:, c].astype(jnp.float32) * gain) - att * sums[1]
        grad = grad.astype(do_ref.dtype)
        do_ref[:, c] = grad
        delta = jnp.sum(grad.astype(jnp.float32) * att, axis=-1, keepdims=True)
        stat_col[1] = jnp.where(lane == h, delta, stat_col[1])

    def norm_group(g):
        loop(per_group, lambda i: norm_head(g * per_group + i))

    loop(GROUPS, norm_group)
    for i in range(2):
        stat_own[i] = jnp.transpose(stat_col[i])[:hp]

    def stat_copy(slot):
        return copy(
            stat_own, stat_buf.at[slot], stat_send.at[slot], stat_recv.at[slot], s - slot - 1
        )

    for slot in range(2):
        @pl.when(s >= slot + 1)
        def _():
            stat_copy(slot).start()
    def query_head(h):
        c = head_cols(h)
        grad = do_ref[:, c]
        delta = jnp.sum(grad.astype(jnp.float32) * att_ref[:, c], axis=-1, keepdims=True)
        dq = jnp.zeros((rows, HS), jnp.float32)
        for j in range(2):
            w = w_ref[h, :, spans[j]].astype(jnp.float32)
            ds = (w * (nt_dot(grad, values_of(j, c)) - delta)).astype(jnp.bfloat16)
            dq = dq + nn_dot(ds, keys_of(j, c))
        dq_ref[:, c] = (dq * scale).astype(dq_ref.dtype)

    def key_terms(h, q, grad, mask, log_total, delta):
        c = head_cols(h)
        w = jnp.exp2(nt_dot(k_ref[:, c], q) * scale2 + mask - log_total)
        ds = (w * (nt_dot(v_ref[:, c], grad) - delta)).astype(jnp.bfloat16)
        return nn_dot(ds, q), nn_dot(w.astype(jnp.bfloat16), grad)

    def local_head(h):
        c = head_cols(h)
        query_head(h)
        log_total, delta = [stat_own[i, pl.ds(h, 1), :] for i in range(2)]
        dk, dv = key_terms(h, q_ref[:, c], do_ref[:, c], bias_t_ref[:, spans[0]], log_total, delta)
        dk_acc[:, c] = dk
        dv_acc[:, c] = dv

    def remote_head(h):
        c = head_cols(h)
        q, grad = [qo_buf[a, :, :, c].reshape(2 * rows, HS) for a in range(2)]
        log_total, delta = [
            jnp.concatenate([stat_buf[j, i, pl.ds(h, 1), :] for j in range(2)], axis=1)
            for i in range(2)
        ]
        dk, dv = key_terms(h, q, grad, bias_t_ref[:, spans[1]], log_total, delta)
        dk_ref[:, c] = ((dk_acc[:, c] + dk) * scale).astype(dk_ref.dtype)
        dv_ref[:, c] = (dv_acc[:, c] + dv).astype(dv_ref.dtype)

    for k in range(2):
        qo_pass(k)

    def local_group(g):
        for i in range(per_group):
            local_head(g * per_group + i)
            if i < 2:
                qo_pass(2 * g + 2 + i)

    half = GROUPS // 2
    loop(half, local_group)

    for slot in range(2):
        @pl.when(s + slot + 1 < n)
        def _():
            copy(
                stat_own, stat_buf.at[slot], stat_send.at[slot], stat_recv.at[slot], s
            ).wait_recv()

    def remote_group(g):
        qo_near_arrive(g)
        loop(per_group, lambda i: remote_head(g * per_group + i))

    def both_groups(i):
        local_group(half + i)
        loop(2, lambda j: remote_group(2 * i + j))

    loop(half, both_groups)

    for slot in range(2):
        @pl.when(s >= slot + 1)
        def _():
            stat_copy(slot).wait_send()

    def sent(g):
        for a in range(2):
            @pl.when(odd & (s >= 3))
            def _():
                kv_copy(a, 0, g, kv_src[a], s).wait_send()

            @pl.when(even & (s + 2 < n))
            def _():
                qo_copy(a, 0, g, qo_src[a], s).wait_send()

    loop(GROUPS, sent)


def body(n, tp, queries, keys, values, cotangent, doc_ids, gain):
    rows, cols = queries.shape
    heads = cols // HS
    hp = -(-heads // 8) * 8
    vmem = pl.BlockSpec(memory_space=pltpu.VMEM)
    bf16, f32 = jnp.bfloat16, jnp.float32
    dma = pltpu.SemaphoreType.DMA
    out = jax.ShapeDtypeStruct((rows, cols), bf16)
    return pl.pallas_call(
        functools.partial(kernel, n, tp),
        out_shape=(out,) * 4,
        in_specs=[vmem] * 6,
        out_specs=(vmem,) * 4,
        scratch_shapes=[
            pltpu.VMEM((2, 2, rows, cols), bf16),
            pltpu.VMEM((2, 2, rows, cols), bf16),
            pltpu.VMEM((rows, cols), bf16),
            pltpu.VMEM((rows, cols), f32),
            pltpu.VMEM((heads, rows, 3 * rows), bf16),
            pltpu.VMEM((rows, 3 * rows), f32),
            pltpu.VMEM((rows, 3 * rows), f32),
            pltpu.VMEM((rows, cols), f32),
            pltpu.VMEM((rows, cols), f32),
            pltpu.VMEM((8, rows), jnp.int32),
            pltpu.VMEM((4, 8, rows), jnp.int32),
            pltpu.VMEM((2, rows, HS), f32),
            pltpu.VMEM((max(tp - 1, 1), 2, rows, HS), f32),
            pltpu.VMEM((2, rows, HS), f32),
            pltpu.VMEM((2, hp, rows), f32),
            pltpu.VMEM((2, 2, hp, rows), f32),
            dma((2, 2, GROUPS)),
            dma((2, 2, GROUPS)),
            dma((2, 2, GROUPS)),
            dma((2, 2, GROUPS)),
            dma((4,)),
            dma((4,)),
            dma((max(tp - 1, 1),)),
            dma((max(tp - 1, 1),)),
            dma((2,)),
            dma((2,)),
        ],
        compiler_params=pltpu.CompilerParams(
            collective_id=0, has_side_effects=True, vmem_limit_bytes=60 * 1024 * 1024
        ),
        cost_estimate=pl.CostEstimate(
            flops=16 * heads * 3 * rows * rows * HS,
            bytes_accessed=16 * rows * cols,
            transcendentals=6 * heads * rows * rows,
        ),
    )(queries, keys, values, cotangent, doc_ids.reshape(1, rows), gain.reshape(1, cols))


def solution(mesh):
    wide = P("section", "tp")
    return jax.shard_map(
        functools.partial(body, mesh.shape["section"], mesh.shape["tp"]),
        mesh=mesh,
        in_specs=(wide, wide, wide, wide, P("section"), P("tp")),
        out_specs=(wide,) * 4,
        check_vma=False,
    )
```

```python
import functools
import math

import jax
import jax.numpy as jnp
from jax import lax
from jax.experimental import pallas as pl
from jax.experimental.pallas import tpu as pltpu
from jax.sharding import PartitionSpec as P

HS = 128
GROUPS = 6
DEPTH = 3
MESH = pl.DeviceIdType.MESH
LOG2E = math.log2(math.e)
HIDDEN = -1e30
NT = (((1,), (1,)), ((), ()))


def nt_dot(a, b):
    return lax.dot_general(a, b, NT, preferred_element_type=jnp.float32)


def nn_dot(a, b):
    return jnp.dot(a, b, preferred_element_type=jnp.float32)


def kernel(
    n,
    tp,
    q_ref,
    k_ref,
    v_ref,
    cot_ref,
    doc_ref,
    gain_ref,
    normed_ref,
    dq_ref,
    dk_ref,
    dv_ref,
    kv_buf,
    qo_buf,
    do_ref,
    att_ref,
    w_ref,
    bias_ref,
    bias_t_ref,
    dk_acc,
    dv_acc,
    doc_own,
    doc_buf,
    sums,
    sums_buf,
    stat_col,
    stat_own,
    stat_buf,
    kv_send,
    kv_recv,
    qo_send,
    qo_recv,
    doc_send,
    doc_recv,
    sums_send,
    sums_recv,
    stat_send,
    stat_recv,
):
    rows, cols = q_ref.shape
    heads = cols // HS
    per_group = heads // GROUPS
    width = per_group * HS
    features = cols * tp
    scale = HS ** (-0.5)
    scale2 = scale * LOG2E
    hp = stat_own.shape[1]
    s = lax.axis_index("section")
    t = lax.axis_index("tp")
    odd = lax.rem(s, 2) == 1
    even = lax.rem(s, 2) == 0

    def copy(src, dst, send, recv, section):
        return pltpu.make_async_remote_copy(
            src_ref=src,
            dst_ref=dst,
            send_sem=send,
            recv_sem=recv,
            device_id={"section": section},
            device_id_type=MESH,
        )

    def group_cols(g):
        return pl.ds(pl.multiple_of(g * width, HS), width)

    def head_cols(h):
        return pl.ds(pl.multiple_of(h * HS, HS), HS)

    near = [(-1, s >= 1), (-2, s >= 2), (1, s + 1 < n), (2, s + 2 < n)]

    barrier = pltpu.get_barrier_semaphore()
    for step, there in near:
        @pl.when(there)
        def _():
            pl.semaphore_signal(
                barrier, inc=1, device_id={"section": s + step}, device_id_type=MESH
            )
    for j in range(1, tp):
        pl.semaphore_signal(
            barrier, inc=1, device_id={"tp": lax.rem(t + j, tp)}, device_id_type=MESH
        )
    pl.semaphore_wait(barrier, jnp.minimum(s, 2) + jnp.minimum(n - 1 - s, 2) + tp - 1)

    doc_own[...] = jnp.broadcast_to(doc_ref[...], doc_own.shape)
    back = [2, 3, 0, 1]

    def doc_copy(i):
        return copy(
            doc_own, doc_buf.at[back[i]], doc_send.at[i], doc_recv.at[back[i]], s + near[i][0]
        )

    for i in range(4):
        @pl.when(near[i][1])
        def _():
            doc_copy(i).start()

    kv_src = (k_ref, v_ref)
    qo_src = (q_ref, do_ref)

    def kv_copy(a, slot, g, src, section):
        c = group_cols(g)
        return copy(
            src.at[:, c], kv_buf.at[a, slot, :, c], kv_send.at[a, slot, g],
            kv_recv.at[a, slot, g], section,
        )

    def qo_copy(a, slot, g, src, section):
        c = group_cols(g)
        return copy(
            src.at[:, c], qo_buf.at[a, slot, :, c], qo_send.at[a, slot, g],
            qo_recv.at[a, slot, g], section,
        )

    first = lax.rem(t, 2) == 0
    second = lax.rem(t, 2) == 1

    def in_turn(one, other):
        pl.when(one[0] & first)(lambda: one[1]())
        pl.when(other[0])(lambda: other[1]())
        pl.when(one[0] & second)(lambda: one[1]())

    def kv_start(a, g):
        in_turn(
            (even, lambda: kv_copy(a, 0, g, kv_src[a], s + 1).start()),
            (s + 2 < n, lambda: kv_copy(a, 1, g, kv_src[a], s + 2).start()),
        )

    def kv_pass(a, g):
        @pl.when(s >= 2)
        def _():
            kv_copy(a, 1, g, kv_src[a], s).wait_recv()

            @pl.when(odd)
            def _():
                kv_copy(a, 0, g, kv_buf.at[a, 1], s - 1).start()

    def kv_next(a, g):
        @pl.when(even)
        def _():
            kv_copy(a, 0, g, kv_src[a], s).wait_send()

        @pl.when(s + 2 < n)
        def _():
            kv_copy(a, 1, g, kv_src[a], s).wait_send()

        @pl.when(g + DEPTH < GROUPS)
        def _():
            kv_start(a, g + DEPTH)

    def kv_near_arrive(a, g):
        @pl.when(s >= 1)
        def _():
            kv_copy(a, 0, g, kv_src[a], s).wait_recv()

    half = GROUPS // 2

    def qo_start(a, g):
        in_turn(
            (odd, lambda: qo_copy(a, 0, g, qo_src[a], s - 1).start()),
            (s >= 2, lambda: qo_copy(a, 1, g, qo_src[a], s - 2).start()),
        )

    def qo_left(a, g):
        @pl.when(odd)
        def _():
            qo_copy(a, 0, g, qo_src[a], s).wait_send()

        @pl.when(s >= 2)
        def _():
            qo_copy(a, 1, g, qo_src[a], s).wait_send()

    def qo_pass(a, g):
        @pl.when(s + 2 < n)
        def _():
            qo_copy(a, 1, g, qo_src[a], s).wait_recv()

            @pl.when(even)
            def _():
                qo_copy(a, 0, g, qo_buf.at[a, 1], s + 1).start()

    def qo_near_arrive(g):
        @pl.when(s + 1 < n)
        def _():
            for a in range(2):
                qo_copy(a, 0, g, qo_src[a], s).wait_recv()

    def loop(count, f):
        lax.fori_loop(0, count, lambda i, c: (f(i), c)[1], 0)

    for g in range(DEPTH):
        for a in range(2):
            kv_start(a, g)

    for slot in range(2):
        @pl.when(s < slot + 1)
        def _():
            kv_buf[:, slot] = jnp.zeros((2, rows, cols), kv_buf.dtype)
            doc_buf[slot] = jnp.zeros(doc_buf.shape[1:], doc_buf.dtype)

        @pl.when(s + slot + 1 >= n)
        def _():
            qo_buf[:, slot] = jnp.zeros((2, rows, cols), qo_buf.dtype)
            stat_buf[slot] = jnp.zeros(stat_buf.shape[1:], stat_buf.dtype)
            doc_buf[2 + slot] = jnp.zeros(doc_buf.shape[1:], doc_buf.dtype)

    sums[...] = jnp.zeros(sums.shape, sums.dtype)
    stat_col[...] = jnp.zeros(stat_col.shape, stat_col.dtype)

    doc_row = doc_ref[...].astype(jnp.float32)
    doc_col = jnp.transpose(jnp.broadcast_to(doc_row, (HS, rows)))[:, :1]
    for i in range(4):
        @pl.when(near[i][1])
        def _():
            doc_copy(i).wait_send()
            copy(doc_own, doc_buf.at[i], doc_send.at[i], doc_recv.at[i], s).wait_recv()
    down = lax.broadcasted_iota(jnp.int32, (rows, rows), 0)
    across = lax.broadcasted_iota(jnp.int32, (rows, rows), 1)

    spans = (slice(0, rows), slice(rows, 3 * rows))

    def bias(visible):
        return jnp.where(visible, 0.0, HIDDEN)

    same = doc_col == doc_row
    bias_ref[:, spans[0]] = bias(same & (down >= across))
    bias_t_ref[:, spans[0]] = bias(same & (across >= down))
    for i in range(2):
        for ref, slot, where_far in ((bias_ref, i, down < across), (bias_t_ref, i + 2, across < down)):
            other = doc_buf[slot][:1].astype(jnp.float32)
            visible = (doc_col == other) & near[slot][1]
            if i == 1:
                visible = visible & where_far
            ref[:, (i + 1) * rows : (i + 2) * rows] = bias(visible)

    lane = lax.broadcasted_iota(jnp.int32, (rows, HS), 1)

    def keys_of(j, c):
        return k_ref[:, c] if j == 0 else kv_buf[0, :, :, c].reshape(2 * rows, HS)

    def values_of(j, c):
        return v_ref[:, c] if j == 0 else kv_buf[1, :, :, c].reshape(2 * rows, HS)

    def forward_head(h):
        c = head_cols(h)
        q = q_ref[:, c]
        scores = [nt_dot(q, keys_of(j, c)) * scale2 + bias_ref[:, spans[j]] for j in range(2)]
        top = jnp.maximum(
            jnp.max(scores[0], axis=-1, keepdims=True), jnp.max(scores[1], axis=-1, keepdims=True)
        )
        parts = [jnp.exp2(x - top) for x in scores]
        total = jnp.sum(parts[0], axis=-1, keepdims=True) + jnp.sum(
            parts[1], axis=-1, keepdims=True
        )
        recip = 1.0 / total
        att = jnp.zeros((rows, HS), jnp.float32)
        for j in range(2):
            w = (parts[j] * recip).astype(jnp.bfloat16)
            w_ref[h, :, spans[j]] = w
            att = att + nn_dot(w, values_of(j, c))
        att_ref[:, c] = att
        stat_col[0] = jnp.where(lane == h, top + jnp.log2(total), stat_col[0])
        sums[0] += att * att
        sums[1] += cot_ref[:, c].astype(jnp.float32) * gain_ref[:, c] * att

    def forward_group(g):
        @pl.when(g < GROUPS)
        def _():
            for a in range(2):
                kv_pass(a, g)
            for a in range(2):
                kv_next(a, g)

        @pl.when(g == GROUPS - 1)
        def _():
            loop(GROUPS, lambda i: qo_start(0, i))

        @pl.when(g >= 1)
        def _():
            for a in range(2):
                kv_near_arrive(a, g - 1)
            loop(per_group, lambda i: forward_head((g - 1) * per_group + i))

    loop(GROUPS + 1, forward_group)

    def sums_copy(j):
        return pltpu.make_async_remote_copy(
            src_ref=sums,
            dst_ref=sums_buf.at[j - 1],
            send_sem=sums_send.at[j - 1],
            recv_sem=sums_recv.at[j - 1],
            device_id={"tp": lax.rem(t + j, tp)},
            device_id_type=MESH,
        )

    for j in range(1, tp):
        sums_copy(j).start()
    squares, inner = sums[0], sums[1]
    for j in range(1, tp):
        sums_copy(j).wait()
        squares = squares + sums_buf[j - 1, 0]
        inner = inner + sums_buf[j - 1, 1]
    inverse = lax.rsqrt(jnp.sum(squares, axis=-1, keepdims=True) / features + 1e-05)
    factor = inverse * inverse * inverse * jnp.sum(inner, axis=-1, keepdims=True) / features
    sums[0] = jnp.broadcast_to(inverse, (rows, HS))
    sums[1] = jnp.broadcast_to(factor, (rows, HS))

    def norm_head(h):
        c = head_cols(h)
        att = att_ref[:, c]
        gain = gain_ref[:, c]
        normed_ref[:, c] = (att * sums[0] * gain).astype(normed_ref.dtype)
        grad = sums[0] * (cot_ref[:, c].astype(jnp.float32) * gain) - att * sums[1]
        grad = grad.astype(do_ref.dtype)
        do_ref[:, c] = grad
        delta = jnp.sum(grad.astype(jnp.float32) * att, axis=-1, keepdims=True)
        stat_col[1] = jnp.where(lane == h, delta, stat_col[1])

    def norm_group(g):
        loop(per_group, lambda i: norm_head(g * per_group + i))
        pl.when(g < half)(lambda: qo_start(1, g))

    loop(GROUPS, norm_group)
    for i in range(2):
        stat_own[i] = jnp.transpose(stat_col[i])[:hp]

    def stat_copy(slot):
        return copy(
            stat_own, stat_buf.at[slot], stat_send.at[slot], stat_recv.at[slot], s - slot - 1
        )

    for slot in range(2):
        @pl.when(s >= slot + 1)
        def _():
            stat_copy(slot).start()
    def query_head(h):
        c = head_cols(h)
        grad = do_ref[:, c]
        delta = jnp.sum(grad.astype(jnp.float32) * att_ref[:, c], axis=-1, keepdims=True)
        dq = jnp.zeros((rows, HS), jnp.float32)
        for j in range(2):
            w = w_ref[h, :, spans[j]].astype(jnp.float32)
            ds = (w * (nt_dot(grad, values_of(j, c)) - delta)).astype(jnp.bfloat16)
            dq = dq + nn_dot(ds, keys_of(j, c))
        dq_ref[:, c] = (dq * scale).astype(dq_ref.dtype)

    def key_terms(h, q, grad, mask, log_total, delta):
        c = head_cols(h)
        w = jnp.exp2(nt_dot(k_ref[:, c], q) * scale2 + mask - log_total)
        ds = (w * (nt_dot(v_ref[:, c], grad) - delta)).astype(jnp.bfloat16)
        return nn_dot(ds, q), nn_dot(w.astype(jnp.bfloat16), grad)

    def local_head(h):
        c = head_cols(h)
        query_head(h)
        log_total, delta = [stat_own[i, pl.ds(h, 1), :] for i in range(2)]
        dk, dv = key_terms(h, q_ref[:, c], do_ref[:, c], bias_t_ref[:, spans[0]], log_total, delta)
        dk_acc[:, c] = dk
        dv_acc[:, c] = dv

    def remote_head(h):
        c = head_cols(h)
        q, grad = [qo_buf[a, :, :, c].reshape(2 * rows, HS) for a in range(2)]
        log_total, delta = [
            jnp.concatenate([stat_buf[j, i, pl.ds(h, 1), :] for j in range(2)], axis=1)
            for i in range(2)
        ]
        dk, dv = key_terms(h, q, grad, bias_t_ref[:, spans[1]], log_total, delta)
        dk_ref[:, c] = ((dk_acc[:, c] + dk) * scale).astype(dk_ref.dtype)
        dv_ref[:, c] = (dv_acc[:, c] + dv).astype(dv_ref.dtype)

    def second_half(i):
        qo_left(1, i)
        qo_start(1, i + half)

    def local_group(g):
        loop(per_group, lambda i: local_head(g * per_group + i))
        pl.when(g == 1)(lambda: loop(half, lambda i: qo_pass(0, i)))
        pl.when(g == 2)(lambda: loop(half, lambda i: qo_pass(0, half + i)))

        @pl.when(g == GROUPS - 2)
        def _():
            loop(half, second_half)
            loop(half, lambda i: qo_pass(1, i))

    loop(GROUPS, local_group)

    for slot in range(2):
        @pl.when(s + slot + 1 < n)
        def _():
            copy(
                stat_own, stat_buf.at[slot], stat_send.at[slot], stat_recv.at[slot], s
            ).wait_recv()

    def remote_group(g):
        pl.when(g == 1)(lambda: loop(half, lambda i: qo_pass(1, half + i)))
        qo_near_arrive(g)
        loop(per_group, lambda i: remote_head(g * per_group + i))

    loop(GROUPS, remote_group)

    for slot in range(2):
        @pl.when(s >= slot + 1)
        def _():
            stat_copy(slot).wait_send()

    def sent(g):
        for a in range(2):
            @pl.when(odd & (s >= 3))
            def _():
                kv_copy(a, 0, g, kv_src[a], s).wait_send()

            @pl.when(even & (s + 2 < n))
            def _():
                qo_copy(a, 0, g, qo_src[a], s).wait_send()

        qo_left(0, g)
        pl.when(g >= half)(lambda: qo_left(1, g))

    loop(GROUPS, sent)


def body(n, tp, queries, keys, values, cotangent, doc_ids, gain):
    rows, cols = queries.shape
    heads = cols // HS
    hp = -(-heads // 8) * 8
    vmem = pl.BlockSpec(memory_space=pltpu.VMEM)
    bf16, f32 = jnp.bfloat16, jnp.float32
    dma = pltpu.SemaphoreType.DMA
    out = jax.ShapeDtypeStruct((rows, cols), bf16)
    return pl.pallas_call(
        functools.partial(kernel, n, tp),
        out_shape=(out,) * 4,
        in_specs=[vmem] * 6,
        out_specs=(vmem,) * 4,
        scratch_shapes=[
            pltpu.VMEM((2, 2, rows, cols), bf16),
            pltpu.VMEM((2, 2, rows, cols), bf16),
            pltpu.VMEM((rows, cols), bf16),
            pltpu.VMEM((rows, cols), f32),
            pltpu.VMEM((heads, rows, 3 * rows), bf16),
            pltpu.VMEM((rows, 3 * rows), f32),
            pltpu.VMEM((rows, 3 * rows), f32),
            pltpu.VMEM((rows, cols), f32),
            pltpu.VMEM((rows, cols), f32),
            pltpu.VMEM((8, rows), jnp.int32),
            pltpu.VMEM((4, 8, rows), jnp.int32),
            pltpu.VMEM((2, rows, HS), f32),
            pltpu.VMEM((max(tp - 1, 1), 2, rows, HS), f32),
            pltpu.VMEM((2, rows, HS), f32),
            pltpu.VMEM((2, hp, rows), f32),
            pltpu.VMEM((2, 2, hp, rows), f32),
            dma((2, 2, GROUPS)),
            dma((2, 2, GROUPS)),
            dma((2, 2, GROUPS)),
            dma((2, 2, GROUPS)),
            dma((4,)),
            dma((4,)),
            dma((max(tp - 1, 1),)),
            dma((max(tp - 1, 1),)),
            dma((2,)),
            dma((2,)),
        ],
        compiler_params=pltpu.CompilerParams(
            collective_id=0, has_side_effects=True, vmem_limit_bytes=60 * 1024 * 1024
        ),
        cost_estimate=pl.CostEstimate(
            flops=16 * heads * 3 * rows * rows * HS,
            bytes_accessed=16 * rows * cols,
            transcendentals=6 * heads * rows * rows,
        ),
    )(queries, keys, values, cotangent, doc_ids.reshape(1, rows), gain.reshape(1, cols))


def solution(mesh):
    wide = P("section", "tp")
    return jax.shard_map(
        functools.partial(body, mesh.shape["section"], mesh.shape["tp"]),
        mesh=mesh,
        in_specs=(wide, wide, wide, wide, P("section"), P("tp")),
        out_specs=(wide,) * 4,
        check_vma=False,
    )
```

```python
import functools
import math

import jax
import jax.numpy as jnp
from jax import lax
from jax.experimental import pallas as pl
from jax.experimental.pallas import tpu as pltpu
from jax.sharding import PartitionSpec as P

HS = 128
GROUPS = 6
PASSED = 3
MESH = pl.DeviceIdType.MESH
LOG2E = math.log2(math.e)
HIDDEN = -1e30
NT = (((1,), (1,)), ((), ()))


def nt_dot(a, b):
    return lax.dot_general(a, b, NT, preferred_element_type=jnp.float32)


def nn_dot(a, b):
    return jnp.dot(a, b, preferred_element_type=jnp.float32)


def kernel(
    n,
    tp,
    q_ref,
    k_ref,
    v_ref,
    cot_ref,
    doc_ref,
    gain_ref,
    normed_ref,
    dq_ref,
    dk_ref,
    dv_ref,
    kv_buf,
    qo_buf,
    do_ref,
    att_ref,
    w_ref,
    bias_ref,
    bias_t_ref,
    dk_acc,
    dv_acc,
    doc_own,
    doc_buf,
    sums,
    sums_buf,
    stat_col,
    stat_own,
    stat_buf,
    kv_send,
    kv_recv,
    qo_send,
    qo_recv,
    doc_send,
    doc_recv,
    sums_send,
    sums_recv,
    stat_send,
    stat_recv,
):
    rows, cols = q_ref.shape
    heads = cols // HS
    per_group = heads // GROUPS
    width = per_group * HS
    features = cols * tp
    scale = HS ** (-0.5)
    scale2 = scale * LOG2E
    hp = stat_own.shape[1]
    s = lax.axis_index("section")
    t = lax.axis_index("tp")
    odd = lax.rem(s, 2) == 1
    even = lax.rem(s, 2) == 0

    def copy(src, dst, send, recv, section):
        return pltpu.make_async_remote_copy(
            src_ref=src,
            dst_ref=dst,
            send_sem=send,
            recv_sem=recv,
            device_id={"section": section},
            device_id_type=MESH,
        )

    def group_cols(g):
        return pl.ds(pl.multiple_of(g * width, HS), width)

    def head_cols(h):
        return pl.ds(pl.multiple_of(h * HS, HS), HS)

    near = [(-1, s >= 1), (-2, s >= 2), (1, s + 1 < n), (2, s + 2 < n)]

    barrier = pltpu.get_barrier_semaphore()
    for step, there in near:
        @pl.when(there)
        def _():
            pl.semaphore_signal(
                barrier, inc=1, device_id={"section": s + step}, device_id_type=MESH
            )
    for j in range(1, tp):
        pl.semaphore_signal(
            barrier, inc=1, device_id={"tp": lax.rem(t + j, tp)}, device_id_type=MESH
        )
    pl.semaphore_wait(barrier, jnp.minimum(s, 2) + jnp.minimum(n - 1 - s, 2) + tp - 1)

    doc_own[...] = jnp.broadcast_to(doc_ref[...], doc_own.shape)
    back = [2, 3, 0, 1]

    def doc_copy(i):
        return copy(
            doc_own, doc_buf.at[back[i]], doc_send.at[i], doc_recv.at[back[i]], s + near[i][0]
        )

    for i in range(4):
        @pl.when(near[i][1])
        def _():
            doc_copy(i).start()

    kv_src = (k_ref, v_ref)
    qo_src = (q_ref, do_ref)

    def kv_copy(a, slot, g, src, section):
        c = group_cols(g)
        return copy(
            src.at[:, c], kv_buf.at[a, slot, :, c], kv_send.at[a, slot, g],
            kv_recv.at[a, slot, g], section,
        )

    def qo_copy(a, slot, g, src, section):
        c = group_cols(g)
        return copy(
            src.at[:, c], qo_buf.at[a, slot, :, c], qo_send.at[a, slot, g],
            qo_recv.at[a, slot, g], section,
        )

    def kv_start(g):
        for a in range(2):
            @pl.when(even | ((g >= PASSED) & (s + 2 < n)))
            def _():
                kv_copy(a, 0, g, kv_src[a], s + 1).start()

            @pl.when(s + 2 < n)
            def _():
                kv_copy(a, 1, g, kv_src[a], s + 2).start()

    def qo_start(a, g):
        @pl.when(odd | ((g >= PASSED) & (s >= 2)))
        def _():
            qo_copy(a, 0, g, qo_src[a], s - 1).start()

        @pl.when(s >= 2)
        def _():
            qo_copy(a, 1, g, qo_src[a], s - 2).start()

    def kv_arrive(g):
        @pl.when(s >= 2)
        def _():
            for a in range(2):
                kv_copy(a, 1, g, kv_src[a], s).wait_recv()

                @pl.when(odd & (g < PASSED))
                def _():
                    kv_copy(a, 0, g, kv_buf.at[a, 1], s - 1).start()

        @pl.when(s >= 1)
        def _():
            for a in range(2):
                kv_copy(a, 0, g, kv_src[a], s).wait_recv()

    def qo_far_arrive(a, g):
        @pl.when((s + 2 < n) & (g >= 0) & (g < GROUPS))
        def _():
            qo_copy(a, 1, g, qo_src[a], s).wait_recv()

            @pl.when(even & (g < PASSED))
            def _():
                qo_copy(a, 0, g, qo_buf.at[a, 1], s + 1).start()

    def qo_near_arrive(g):
        @pl.when(s + 1 < n)
        def _():
            for a in range(2):
                qo_copy(a, 0, g, qo_src[a], s).wait_recv()

    def loop(count, f):
        lax.fori_loop(0, count, lambda i, c: (f(i), c)[1], 0)

    loop(GROUPS, kv_start)

    for slot in range(2):
        @pl.when(s < slot + 1)
        def _():
            kv_buf[:, slot] = jnp.zeros((2, rows, cols), kv_buf.dtype)
            doc_buf[slot] = jnp.zeros(doc_buf.shape[1:], doc_buf.dtype)

        @pl.when(s + slot + 1 >= n)
        def _():
            qo_buf[:, slot] = jnp.zeros((2, rows, cols), qo_buf.dtype)
            stat_buf[slot] = jnp.zeros(stat_buf.shape[1:], stat_buf.dtype)
            doc_buf[2 + slot] = jnp.zeros(doc_buf.shape[1:], doc_buf.dtype)

    sums[...] = jnp.zeros(sums.shape, sums.dtype)
    stat_col[...] = jnp.zeros(stat_col.shape, stat_col.dtype)

    doc_row = doc_ref[...].astype(jnp.float32)
    doc_col = jnp.transpose(jnp.broadcast_to(doc_row, (HS, rows)))[:, :1]
    for i in range(4):
        @pl.when(near[i][1])
        def _():
            doc_copy(i).wait_send()
            copy(doc_own, doc_buf.at[i], doc_send.at[i], doc_recv.at[i], s).wait_recv()
    down = lax.broadcasted_iota(jnp.int32, (rows, rows), 0)
    across = lax.broadcasted_iota(jnp.int32, (rows, rows), 1)

    spans = (slice(0, rows), slice(rows, 3 * rows))

    def bias(visible):
        return jnp.where(visible, 0.0, HIDDEN)

    same = doc_col == doc_row
    bias_ref[:, spans[0]] = bias(same & (down >= across))
    bias_t_ref[:, spans[0]] = bias(same & (across >= down))
    for i in range(2):
        for ref, slot, where_far in ((bias_ref, i, down < across), (bias_t_ref, i + 2, across < down)):
            other = doc_buf[slot][:1].astype(jnp.float32)
            visible = (doc_col == other) & near[slot][1]
            if i == 1:
                visible = visible & where_far
            ref[:, (i + 1) * rows : (i + 2) * rows] = bias(visible)

    lane = lax.broadcasted_iota(jnp.int32, (rows, HS), 1)

    def keys_of(j, c):
        return k_ref[:, c] if j == 0 else kv_buf[0, :, :, c].reshape(2 * rows, HS)

    def values_of(j, c):
        return v_ref[:, c] if j == 0 else kv_buf[1, :, :, c].reshape(2 * rows, HS)

    def forward_head(h):
        c = head_cols(h)
        q = q_ref[:, c]
        scores = [nt_dot(q, keys_of(j, c)) * scale2 + bias_ref[:, spans[j]] for j in range(2)]
        top = jnp.maximum(
            jnp.max(scores[0], axis=-1, keepdims=True), jnp.max(scores[1], axis=-1, keepdims=True)
        )
        parts = [jnp.exp2(x - top) for x in scores]
        total = jnp.sum(parts[0], axis=-1, keepdims=True) + jnp.sum(
            parts[1], axis=-1, keepdims=True
        )
        recip = 1.0 / total
        att = jnp.zeros((rows, HS), jnp.float32)
        for j in range(2):
            w = (parts[j] * recip).astype(jnp.bfloat16)
            w_ref[h, :, spans[j]] = w
            att = att + nn_dot(w, values_of(j, c))
        att_ref[:, c] = att
        stat_col[0] = jnp.where(lane == h, top + jnp.log2(total), stat_col[0])
        sums[0] += att * att
        sums[1] += cot_ref[:, c].astype(jnp.float32) * gain_ref[:, c] * att

    def forward_group(g):
        kv_arrive(g)

        @pl.when(g == GROUPS - 1)
        def _():
            loop(GROUPS, lambda i: qo_start(0, i))

        loop(per_group, lambda i: forward_head(g * per_group + i))

    loop(GROUPS, forward_group)

    def sums_copy(j):
        return pltpu.make_async_remote_copy(
            src_ref=sums,
            dst_ref=sums_buf.at[j - 1],
            send_sem=sums_send.at[j - 1],
            recv_sem=sums_recv.at[j - 1],
            device_id={"tp": lax.rem(t + j, tp)},
            device_id_type=MESH,
        )

    for j in range(1, tp):
        sums_copy(j).start()
    for g in range(2):
        qo_far_arrive(0, g)
    squares, inner = sums[0], sums[1]
    for j in range(1, tp):
        sums_copy(j).wait()
        squares = squares + sums_buf[j - 1, 0]
        inner = inner + sums_buf[j - 1, 1]
    inverse = lax.rsqrt(jnp.sum(squares, axis=-1, keepdims=True) / features + 1e-05)
    factor = inverse * inverse * inverse * jnp.sum(inner, axis=-1, keepdims=True) / features
    sums[0] = jnp.broadcast_to(inverse, (rows, HS))
    sums[1] = jnp.broadcast_to(factor, (rows, HS))

    def norm_head(h):
        c = head_cols(h)
        att = att_ref[:, c]
        gain = gain_ref[:, c]
        normed_ref[:, c] = (att * sums[0] * gain).astype(normed_ref.dtype)
        grad = sums[0] * (cot_ref[:, c].astype(jnp.float32) * gain) - att * sums[1]
        grad = grad.astype(do_ref.dtype)
        do_ref[:, c] = grad
        delta = jnp.sum(grad.astype(jnp.float32) * att, axis=-1, keepdims=True)
        stat_col[1] = jnp.where(lane == h, delta, stat_col[1])

    def norm_group(g):
        loop(per_group, lambda i: norm_head(g * per_group + i))
        qo_start(1, g)

    loop(GROUPS, norm_group)
    for i in range(2):
        stat_own[i] = jnp.transpose(stat_col[i])[:hp]

    def stat_copy(slot):
        return copy(
            stat_own, stat_buf.at[slot], stat_send.at[slot], stat_recv.at[slot], s - slot - 1
        )

    for slot in range(2):
        @pl.when(s >= slot + 1)
        def _():
            stat_copy(slot).start()
    def query_head(h):
        c = head_cols(h)
        grad = do_ref[:, c]
        delta = jnp.sum(grad.astype(jnp.float32) * att_ref[:, c], axis=-1, keepdims=True)
        dq = jnp.zeros((rows, HS), jnp.float32)
        for j in range(2):
            w = w_ref[h, :, spans[j]].astype(jnp.float32)
            ds = (w * (nt_dot(grad, values_of(j, c)) - delta)).astype(jnp.bfloat16)
            dq = dq + nn_dot(ds, keys_of(j, c))
        dq_ref[:, c] = (dq * scale).astype(dq_ref.dtype)

    def key_terms(h, q, grad, mask, log_total, delta):
        c = head_cols(h)
        w = jnp.exp2(nt_dot(k_ref[:, c], q) * scale2 + mask - log_total)
        ds = (w * (nt_dot(v_ref[:, c], grad) - delta)).astype(jnp.bfloat16)
        return nn_dot(ds, q), nn_dot(w.astype(jnp.bfloat16), grad)

    def local_head(h):
        c = head_cols(h)
        query_head(h)
        log_total, delta = [stat_own[i, pl.ds(h, 1), :] for i in range(2)]
        dk, dv = key_terms(h, q_ref[:, c], do_ref[:, c], bias_t_ref[:, spans[0]], log_total, delta)
        dk_acc[:, c] = dk
        dv_acc[:, c] = dv

    def remote_head(h):
        c = head_cols(h)
        q, grad = [qo_buf[a, :, :, c].reshape(2 * rows, HS) for a in range(2)]
        log_total, delta = [
            jnp.concatenate([stat_buf[j, i, pl.ds(h, 1), :] for j in range(2)], axis=1)
            for i in range(2)
        ]
        dk, dv = key_terms(h, q, grad, bias_t_ref[:, spans[1]], log_total, delta)
        dk_ref[:, c] = ((dk_acc[:, c] + dk) * scale).astype(dk_ref.dtype)
        dv_ref[:, c] = (dv_acc[:, c] + dv).astype(dv_ref.dtype)

    def local_group(g):
        loop(per_group, lambda i: local_head(g * per_group + i))
        qo_far_arrive(0, g + 2)
        qo_far_arrive(1, g - 2)

    loop(GROUPS, local_group)

    for slot in range(2):
        @pl.when(s + slot + 1 < n)
        def _():
            copy(
                stat_own, stat_buf.at[slot], stat_send.at[slot], stat_recv.at[slot], s
            ).wait_recv()


    def remote_group(g):
        qo_far_arrive(1, g + GROUPS - 2)
        qo_near_arrive(g)
        loop(per_group, lambda i: remote_head(g * per_group + i))

    loop(GROUPS, remote_group)

    for slot in range(2):
        @pl.when(s >= slot + 1)
        def _():
            stat_copy(slot).wait_send()

    def sent(g):
        for a in range(2):
            @pl.when(even | ((g < PASSED) & (s >= 3)) | ((g >= PASSED) & (s + 2 < n)))
            def _():
                kv_copy(a, 0, g, kv_src[a], s).wait_send()

            @pl.when(s + 2 < n)
            def _():
                kv_copy(a, 1, g, kv_src[a], s).wait_send()

            @pl.when(odd | ((g < PASSED) & (s + 3 < n)) | ((g >= PASSED) & (s >= 2)))
            def _():
                qo_copy(a, 0, g, qo_src[a], s).wait_send()

            @pl.when(s >= 2)
            def _():
                qo_copy(a, 1, g, qo_src[a], s).wait_send()

    loop(GROUPS, sent)


def body(n, tp, queries, keys, values, cotangent, doc_ids, gain):
    rows, cols = queries.shape
    heads = cols // HS
    hp = -(-heads // 8) * 8
    vmem = pl.BlockSpec(memory_space=pltpu.VMEM)
    bf16, f32 = jnp.bfloat16, jnp.float32
    dma = pltpu.SemaphoreType.DMA
    out = jax.ShapeDtypeStruct((rows, cols), bf16)
    return pl.pallas_call(
        functools.partial(kernel, n, tp),
        out_shape=(out,) * 4,
        in_specs=[vmem] * 6,
        out_specs=(vmem,) * 4,
        scratch_shapes=[
            pltpu.VMEM((2, 2, rows, cols), bf16),
            pltpu.VMEM((2, 2, rows, cols), bf16),
            pltpu.VMEM((rows, cols), bf16),
            pltpu.VMEM((rows, cols), f32),
            pltpu.VMEM((heads, rows, 3 * rows), bf16),
            pltpu.VMEM((rows, 3 * rows), f32),
            pltpu.VMEM((rows, 3 * rows), f32),
            pltpu.VMEM((rows, cols), f32),
            pltpu.VMEM((rows, cols), f32),
            pltpu.VMEM((8, rows), jnp.int32),
            pltpu.VMEM((4, 8, rows), jnp.int32),
            pltpu.VMEM((2, rows, HS), f32),
            pltpu.VMEM((max(tp - 1, 1), 2, rows, HS), f32),
            pltpu.VMEM((2, rows, HS), f32),
            pltpu.VMEM((2, hp, rows), f32),
            pltpu.VMEM((2, 2, hp, rows), f32),
            dma((2, 2, GROUPS)),
            dma((2, 2, GROUPS)),
            dma((2, 2, GROUPS)),
            dma((2, 2, GROUPS)),
            dma((4,)),
            dma((4,)),
            dma((max(tp - 1, 1),)),
            dma((max(tp - 1, 1),)),
            dma((2,)),
            dma((2,)),
        ],
        compiler_params=pltpu.CompilerParams(
            collective_id=0, has_side_effects=True, vmem_limit_bytes=60 * 1024 * 1024
        ),
        cost_estimate=pl.CostEstimate(
            flops=16 * heads * 3 * rows * rows * HS,
            bytes_accessed=16 * rows * cols,
            transcendentals=6 * heads * rows * rows,
        ),
    )(queries, keys, values, cotangent, doc_ids.reshape(1, rows), gain.reshape(1, cols))


def solution(mesh):
    wide = P("section", "tp")
    return jax.shard_map(
        functools.partial(body, mesh.shape["section"], mesh.shape["tp"]),
        mesh=mesh,
        in_specs=(wide, wide, wide, wide, P("section"), P("tp")),
        out_specs=(wide,) * 4,
        check_vma=False,
    )
```

```python
import functools
import math

import jax
import jax.numpy as jnp
from jax import lax
from jax.experimental import pallas as pl
from jax.experimental.pallas import tpu as pltpu
from jax.sharding import PartitionSpec as P

HS = 128
GROUPS = 6
MESH = pl.DeviceIdType.MESH
LOG2E = math.log2(math.e)
HIDDEN = -1e30
NT = (((1,), (1,)), ((), ()))


def nt_dot(a, b):
    return lax.dot_general(a, b, NT, preferred_element_type=jnp.float32)


def nn_dot(a, b):
    return jnp.dot(a, b, preferred_element_type=jnp.float32)


def kernel(
    n,
    tp,
    q_ref,
    k_ref,
    v_ref,
    cot_ref,
    doc_ref,
    gain_ref,
    normed_ref,
    dq_ref,
    dk_ref,
    dv_ref,
    kv_buf,
    qo_buf,
    do_ref,
    att_ref,
    w_ref,
    bias_ref,
    bias_t_ref,
    dk_acc,
    dv_acc,
    doc_own,
    doc_buf,
    sums,
    sums_buf,
    stat_col,
    stat_own,
    stat_buf,
    kv_send,
    kv_recv,
    qo_send,
    qo_recv,
    doc_send,
    doc_recv,
    sums_send,
    sums_recv,
    stat_send,
    stat_recv,
):
    rows, cols = q_ref.shape
    heads = cols // HS
    per_group = heads // GROUPS
    width = per_group * HS
    features = cols * tp
    scale = HS ** (-0.5)
    scale2 = scale * LOG2E
    hp = stat_own.shape[1]
    s = lax.axis_index("section")
    t = lax.axis_index("tp")
    odd = lax.rem(s, 2) == 1
    even = lax.rem(s, 2) == 0

    def copy(src, dst, send, recv, section):
        return pltpu.make_async_remote_copy(
            src_ref=src,
            dst_ref=dst,
            send_sem=send,
            recv_sem=recv,
            device_id={"section": section},
            device_id_type=MESH,
        )

    def group_cols(g):
        return pl.ds(pl.multiple_of(g * width, HS), width)

    def head_cols(h):
        return pl.ds(pl.multiple_of(h * HS, HS), HS)

    near = [(-1, s >= 1), (-2, s >= 2), (1, s + 1 < n), (2, s + 2 < n)]

    barrier = pltpu.get_barrier_semaphore()
    for step, there in near:
        @pl.when(there)
        def _():
            pl.semaphore_signal(
                barrier, inc=1, device_id={"section": s + step}, device_id_type=MESH
            )
    for j in range(1, tp):
        pl.semaphore_signal(
            barrier, inc=1, device_id={"tp": lax.rem(t + j, tp)}, device_id_type=MESH
        )
    pl.semaphore_wait(barrier, jnp.minimum(s, 2) + jnp.minimum(n - 1 - s, 2) + tp - 1)

    doc_own[...] = jnp.broadcast_to(doc_ref[...], doc_own.shape)
    back = [2, 3, 0, 1]

    def doc_copy(i):
        return copy(
            doc_own, doc_buf.at[back[i]], doc_send.at[i], doc_recv.at[back[i]], s + near[i][0]
        )

    for i in range(4):
        @pl.when(near[i][1])
        def _():
            doc_copy(i).start()

    kv_src = (k_ref, v_ref)
    qo_src = (q_ref, do_ref)

    def kv_copy(a, slot, g, src, section):
        c = group_cols(g)
        return copy(
            src.at[:, c], kv_buf.at[a, slot, :, c], kv_send.at[a, slot, g],
            kv_recv.at[a, slot, g], section,
        )

    def qo_copy(a, slot, g, src, section):
        c = group_cols(g)
        return copy(
            src.at[:, c], qo_buf.at[a, slot, :, c], qo_send.at[a, slot, g],
            qo_recv.at[a, slot, g], section,
        )

    def kv_start(g):
        for a in range(2):
            @pl.when(even)
            def _():
                kv_copy(a, 0, g, kv_src[a], s + 1).start()

            @pl.when(s + 2 < n)
            def _():
                kv_copy(a, 1, g, kv_src[a], s + 2).start()

    def qo_start(a, g):
        @pl.when(odd)
        def _():
            qo_copy(a, 0, g, qo_src[a], s - 1).start()

        @pl.when(s >= 2)
        def _():
            qo_copy(a, 1, g, qo_src[a], s - 2).start()

    def kv_pass(g):
        @pl.when(s >= 2)
        def _():
            for a in range(2):
                kv_copy(a, 1, g, kv_src[a], s).wait_recv()
                kv_copy(a, 0, g, kv_buf.at[a, 1], s - 1).start()

    def kv_arrive(g):
        @pl.when(even & (s >= 2))
        def _():
            for a in range(2):
                kv_copy(a, 1, g, kv_src[a], s).wait_recv()

        @pl.when(s >= 1)
        def _():
            for a in range(2):
                kv_copy(a, 0, g, kv_src[a], s).wait_recv()

    def qo_far_arrive(a, g):
        @pl.when((s + 2 < n) & (g >= 0) & (g < GROUPS))
        def _():
            qo_copy(a, 1, g, qo_src[a], s).wait_recv()

            @pl.when(even)
            def _():
                qo_copy(a, 0, g, qo_buf.at[a, 1], s + 1).start()

    def qo_near_arrive(g):
        @pl.when(s + 1 < n)
        def _():
            for a in range(2):
                qo_copy(a, 0, g, qo_src[a], s).wait_recv()

    def loop(count, f):
        lax.fori_loop(0, count, lambda i, c: (f(i), c)[1], 0)

    half = GROUPS // 2
    loop(half, kv_start)
    pl.when(even)(lambda: loop(half, lambda i: kv_start(half + i)))

    for slot in range(2):
        @pl.when(s < slot + 1)
        def _():
            kv_buf[:, slot] = jnp.zeros((2, rows, cols), kv_buf.dtype)
            doc_buf[slot] = jnp.zeros(doc_buf.shape[1:], doc_buf.dtype)

        @pl.when(s + slot + 1 >= n)
        def _():
            qo_buf[:, slot] = jnp.zeros((2, rows, cols), qo_buf.dtype)
            stat_buf[slot] = jnp.zeros(stat_buf.shape[1:], stat_buf.dtype)
            doc_buf[2 + slot] = jnp.zeros(doc_buf.shape[1:], doc_buf.dtype)

    sums[...] = jnp.zeros(sums.shape, sums.dtype)
    stat_col[...] = jnp.zeros(stat_col.shape, stat_col.dtype)

    doc_row = doc_ref[...].astype(jnp.float32)
    doc_col = jnp.transpose(jnp.broadcast_to(doc_row, (HS, rows)))[:, :1]
    for i in range(4):
        @pl.when(near[i][1])
        def _():
            doc_copy(i).wait_send()
            copy(doc_own, doc_buf.at[i], doc_send.at[i], doc_recv.at[i], s).wait_recv()
    down = lax.broadcasted_iota(jnp.int32, (rows, rows), 0)
    across = lax.broadcasted_iota(jnp.int32, (rows, rows), 1)

    spans = (slice(0, rows), slice(rows, 3 * rows))

    def bias(visible):
        return jnp.where(visible, 0.0, HIDDEN)

    same = doc_col == doc_row
    bias_ref[:, spans[0]] = bias(same & (down >= across))
    bias_t_ref[:, spans[0]] = bias(same & (across >= down))
    for i in range(2):
        for ref, slot, where_far in ((bias_ref, i, down < across), (bias_t_ref, i + 2, across < down)):
            other = doc_buf[slot][:1].astype(jnp.float32)
            visible = (doc_col == other) & near[slot][1]
            if i == 1:
                visible = visible & where_far
            ref[:, (i + 1) * rows : (i + 2) * rows] = bias(visible)

    lane = lax.broadcasted_iota(jnp.int32, (rows, HS), 1)

    def keys_of(j, c):
        return k_ref[:, c] if j == 0 else kv_buf[0, :, :, c].reshape(2 * rows, HS)

    def values_of(j, c):
        return v_ref[:, c] if j == 0 else kv_buf[1, :, :, c].reshape(2 * rows, HS)

    def forward_head(h):
        c = head_cols(h)
        q = q_ref[:, c]
        scores = [nt_dot(q, keys_of(j, c)) * scale2 + bias_ref[:, spans[j]] for j in range(2)]
        top = jnp.maximum(
            jnp.max(scores[0], axis=-1, keepdims=True), jnp.max(scores[1], axis=-1, keepdims=True)
        )
        parts = [jnp.exp2(x - top) for x in scores]
        total = jnp.sum(parts[0], axis=-1, keepdims=True) + jnp.sum(
            parts[1], axis=-1, keepdims=True
        )
        recip = 1.0 / total
        att = jnp.zeros((rows, HS), jnp.float32)
        for j in range(2):
            w = (parts[j] * recip).astype(jnp.bfloat16)
            w_ref[h, :, spans[j]] = w
            att = att + nn_dot(w, values_of(j, c))
        att_ref[:, c] = att
        stat_col[0] = jnp.where(lane == h, top + jnp.log2(total), stat_col[0])
        sums[0] += att * att
        sums[1] += cot_ref[:, c].astype(jnp.float32) * gain_ref[:, c] * att

    def forward_group(g):
        kv_arrive(g)

        @pl.when(g == GROUPS - 1)
        def _():
            loop(GROUPS, lambda i: qo_start(0, i))

        loop(per_group, lambda i: forward_head(g * per_group + i))

    @pl.when(odd)
    def _():
        loop(half, kv_pass)
        loop(half, lambda i: kv_start(half + i))
        loop(half, lambda i: kv_pass(half + i))

    loop(GROUPS, forward_group)

    def sums_copy(j):
        return pltpu.make_async_remote_copy(
            src_ref=sums,
            dst_ref=sums_buf.at[j - 1],
            send_sem=sums_send.at[j - 1],
            recv_sem=sums_recv.at[j - 1],
            device_id={"tp": lax.rem(t + j, tp)},
            device_id_type=MESH,
        )

    for j in range(1, tp):
        sums_copy(j).start()
    for g in range(2):
        qo_far_arrive(0, g)
    squares, inner = sums[0], sums[1]
    for j in range(1, tp):
        sums_copy(j).wait()
        squares = squares + sums_buf[j - 1, 0]
        inner = inner + sums_buf[j - 1, 1]
    inverse = lax.rsqrt(jnp.sum(squares, axis=-1, keepdims=True) / features + 1e-05)
    factor = inverse * inverse * inverse * jnp.sum(inner, axis=-1, keepdims=True) / features
    sums[0] = jnp.broadcast_to(inverse, (rows, HS))
    sums[1] = jnp.broadcast_to(factor, (rows, HS))

    def norm_head(h):
        c = head_cols(h)
        att = att_ref[:, c]
        gain = gain_ref[:, c]
        normed_ref[:, c] = (att * sums[0] * gain).astype(normed_ref.dtype)
        grad = sums[0] * (cot_ref[:, c].astype(jnp.float32) * gain) - att * sums[1]
        grad = grad.astype(do_ref.dtype)
        do_ref[:, c] = grad
        delta = jnp.sum(grad.astype(jnp.float32) * att, axis=-1, keepdims=True)
        stat_col[1] = jnp.where(lane == h, delta, stat_col[1])

    def norm_group(g):
        loop(per_group, lambda i: norm_head(g * per_group + i))
        qo_start(1, g)

    loop(GROUPS, norm_group)
    for i in range(2):
        stat_own[i] = jnp.transpose(stat_col[i])[:hp]

    def stat_copy(slot):
        return copy(
            stat_own, stat_buf.at[slot], stat_send.at[slot], stat_recv.at[slot], s - slot - 1
        )

    for slot in range(2):
        @pl.when(s >= slot + 1)
        def _():
            stat_copy(slot).start()
    def query_head(h):
        c = head_cols(h)
        grad = do_ref[:, c]
        delta = jnp.sum(grad.astype(jnp.float32) * att_ref[:, c], axis=-1, keepdims=True)
        dq = jnp.zeros((rows, HS), jnp.float32)
        for j in range(2):
            w = w_ref[h, :, spans[j]].astype(jnp.float32)
            ds = (w * (nt_dot(grad, values_of(j, c)) - delta)).astype(jnp.bfloat16)
            dq = dq + nn_dot(ds, keys_of(j, c))
        dq_ref[:, c] = (dq * scale).astype(dq_ref.dtype)

    def key_terms(h, q, grad, mask, log_total, delta):
        c = head_cols(h)
        w = jnp.exp2(nt_dot(k_ref[:, c], q) * scale2 + mask - log_total)
        ds = (w * (nt_dot(v_ref[:, c], grad) - delta)).astype(jnp.bfloat16)
        return nn_dot(ds, q), nn_dot(w.astype(jnp.bfloat16), grad)

    def local_head(h):
        c = head_cols(h)
        query_head(h)
        log_total, delta = [stat_own[i, pl.ds(h, 1), :] for i in range(2)]
        dk, dv = key_terms(h, q_ref[:, c], do_ref[:, c], bias_t_ref[:, spans[0]], log_total, delta)
        dk_acc[:, c] = dk
        dv_acc[:, c] = dv

    def remote_head(h):
        c = head_cols(h)
        q, grad = [qo_buf[a, :, :, c].reshape(2 * rows, HS) for a in range(2)]
        log_total, delta = [
            jnp.concatenate([stat_buf[j, i, pl.ds(h, 1), :] for j in range(2)], axis=1)
            for i in range(2)
        ]
        dk, dv = key_terms(h, q, grad, bias_t_ref[:, spans[1]], log_total, delta)
        dk_ref[:, c] = ((dk_acc[:, c] + dk) * scale).astype(dk_ref.dtype)
        dv_ref[:, c] = (dv_acc[:, c] + dv).astype(dv_ref.dtype)

    def local_group(g):
        loop(per_group, lambda i: local_head(g * per_group + i))
        qo_far_arrive(0, g + 2)
        qo_far_arrive(1, g - 2)

    loop(GROUPS, local_group)

    for slot in range(2):
        @pl.when(s + slot + 1 < n)
        def _():
            copy(
                stat_own, stat_buf.at[slot], stat_send.at[slot], stat_recv.at[slot], s
            ).wait_recv()


    def remote_group(g):
        qo_far_arrive(1, g + GROUPS - 2)
        qo_near_arrive(g)
        loop(per_group, lambda i: remote_head(g * per_group + i))

    loop(GROUPS, remote_group)

    for slot in range(2):
        @pl.when(s >= slot + 1)
        def _():
            stat_copy(slot).wait_send()

    def sent(g):
        for a in range(2):
            @pl.when(even | (s >= 3))
            def _():
                kv_copy(a, 0, g, kv_src[a], s).wait_send()

            @pl.when(s + 2 < n)
            def _():
                kv_copy(a, 1, g, kv_src[a], s).wait_send()

            @pl.when(odd | (s + 3 < n))
            def _():
                qo_copy(a, 0, g, qo_src[a], s).wait_send()

            @pl.when(s >= 2)
            def _():
                qo_copy(a, 1, g, qo_src[a], s).wait_send()

    loop(GROUPS, sent)


def body(n, tp, queries, keys, values, cotangent, doc_ids, gain):
    rows, cols = queries.shape
    heads = cols // HS
    hp = -(-heads // 8) * 8
    vmem = pl.BlockSpec(memory_space=pltpu.VMEM)
    bf16, f32 = jnp.bfloat16, jnp.float32
    dma = pltpu.SemaphoreType.DMA
    out = jax.ShapeDtypeStruct((rows, cols), bf16)
    return pl.pallas_call(
        functools.partial(kernel, n, tp),
        out_shape=(out,) * 4,
        in_specs=[vmem] * 6,
        out_specs=(vmem,) * 4,
        scratch_shapes=[
            pltpu.VMEM((2, 2, rows, cols), bf16),
            pltpu.VMEM((2, 2, rows, cols), bf16),
            pltpu.VMEM((rows, cols), bf16),
            pltpu.VMEM((rows, cols), f32),
            pltpu.VMEM((heads, rows, 3 * rows), bf16),
            pltpu.VMEM((rows, 3 * rows), f32),
            pltpu.VMEM((rows, 3 * rows), f32),
            pltpu.VMEM((rows, cols), f32),
            pltpu.VMEM((rows, cols), f32),
            pltpu.VMEM((8, rows), jnp.int32),
            pltpu.VMEM((4, 8, rows), jnp.int32),
            pltpu.VMEM((2, rows, HS), f32),
            pltpu.VMEM((max(tp - 1, 1), 2, rows, HS), f32),
            pltpu.VMEM((2, rows, HS), f32),
            pltpu.VMEM((2, hp, rows), f32),
            pltpu.VMEM((2, 2, hp, rows), f32),
            dma((2, 2, GROUPS)),
            dma((2, 2, GROUPS)),
            dma((2, 2, GROUPS)),
            dma((2, 2, GROUPS)),
            dma((4,)),
            dma((4,)),
            dma((max(tp - 1, 1),)),
            dma((max(tp - 1, 1),)),
            dma((2,)),
            dma((2,)),
        ],
        compiler_params=pltpu.CompilerParams(
            collective_id=0, has_side_effects=True, vmem_limit_bytes=60 * 1024 * 1024
        ),
        cost_estimate=pl.CostEstimate(
            flops=16 * heads * 3 * rows * rows * HS,
            bytes_accessed=16 * rows * cols,
            transcendentals=6 * heads * rows * rows,
        ),
    )(queries, keys, values, cotangent, doc_ids.reshape(1, rows), gain.reshape(1, cols))


def solution(mesh):
    wide = P("section", "tp")
    return jax.shard_map(
        functools.partial(body, mesh.shape["section"], mesh.shape["tp"]),
        mesh=mesh,
        in_specs=(wide, wide, wide, wide, P("section"), P("tp")),
        out_specs=(wide,) * 4,
        check_vma=False,
    )
```
